32 devices in a mesh: row: 4 (over y, core), col: 8 (over z, x).
Axes of the slice: x: 2, y: 2, z: 4, core: 2. Of those that a mesh axis runs over, the one named last changes fastest.
Arguments:
- outcome_vectors: bfloat16 [4096, 1024], P('row', 'col'), may hold values from -6 to 6
- u_factor: bfloat16 [32, 1024], P(None, 'col'), may hold values from -0.03125 to 0.03125
- v_factor: bfloat16 [32, 1024], P(None, 'col'), may hold values from -0.03125 to 0.03125
- outcome_index: int32 [4096], replicated, may hold values from 0 to 4095, each once
Outputs:
- factored: float32 [4096, 4096], P('row', 'col')
The draws below stay inside these ranges and needn't reach their ends.
All inputs are finite; a program needn't handle non-finite values.
Results may differ from the reference program's by a relative error of at most 0.0056.
Values may be sent and summed in bfloat16 or wider, within the bound.
No kernel may reach another device: no remote copies, remote signals or barrier semaphores. Data moves between devices by JAX's collectives and lax.ppermute only.
A program may use at most 64 MiB of HBM per device.

```python
import jax
import jax.numpy as jnp
from jax import lax

N_EMB = 1024
R = 32
PANEL = 256
NPANEL = 2
M_ROWS = 4096


def block_levels(key, dims, pieces, smallest, largest):
    def one(position, shards_of):
        steps = jax.random.uniform(jax.random.fold_in(jax.random.fold_in(key, 6), position), (shards_of,), jnp.float32, smallest / len(pieces), largest / len(pieces))
        return jnp.repeat(jnp.exp(steps), dims[position] // shards_of).reshape((-1,) + (1,) * (len(dims) - position - 1))

    factor_of = one(*pieces[0])
    for cut in pieces[1:]:
        factor_of = factor_of * one(*cut)
    return factor_of


def centred(key, shape, width, reach, cuts=(), kind=jnp.bfloat16):
    loudness = block_levels(key, shape, cuts, -0.22, 0.18) if cuts else 1.0
    array = jax.random.normal(key, shape, jnp.float32) * width * loudness
    return jnp.minimum(jnp.maximum(array, -reach), reach).astype(kind)


def setup_inputs(seed: int = 0) -> dict:
    streams_of = jax.random.split(jax.random.key(seed), 5)
    outcome_vectors = centred(streams_of[0], (M_ROWS, N_EMB), 1.0, 6.0, ((0, 4), (1, 8)))
    u_factor = centred(streams_of[1], (R, N_EMB), (N_EMB * R) ** -0.5, 0.03125, ((1, 8),))
    v_factor = centred(streams_of[2], (R, N_EMB), (N_EMB * R) ** -0.5, 0.03125, ((1, 8),))
    outcome_index = jax.random.permutation(streams_of[3], M_ROWS).astype(jnp.int32)
    return dict(outcome_vectors=outcome_vectors, u_factor=u_factor, v_factor=v_factor, outcome_index=outcome_index)


def reference(outcome_vectors, u_factor, v_factor, outcome_index):
    factors = jnp.concatenate([u_factor, v_factor], axis=0)
    transformed = lax.dot_general(outcome_vectors.astype(jnp.float32), factors.astype(jnp.float32), (((1,), (1,)), ((), ())), preferred_element_type=jnp.float32).astype(jnp.bfloat16)
    picked = jnp.take(transformed, outcome_index.astype(jnp.int32), axis=0)
    first = picked[:, :R]
    second = picked[:, R:]
    gram_u = jnp.dot(first.astype(jnp.float32), first.T.astype(jnp.float32), preferred_element_type=jnp.float32)
    gram_v = jnp.dot(second.astype(jnp.float32), second.T.astype(jnp.float32), preferred_element_type=jnp.float32)
    schur = gram_u * gram_v + jnp.eye(M_ROWS, dtype=jnp.float32)
    for step in range(NPANEL):
        start = step * PANEL
        stop = start + PANEL
        lower = jnp.linalg.cholesky(schur[start:stop, start:stop])
        below = jax.scipy.linalg.solve_triangular(lower, schur[stop:, start:stop].T, lower=True).T
        update = jnp.dot(below, below.T, precision=lax.Precision.HIGHEST)
        schur = schur.at[stop:, stop:].add(-update)
        schur = schur.at[start:stop, start:stop].set(jnp.tril(lower))
        schur = schur.at[stop:, start:stop].set(below)
    return schur
```

```python
import jax
import jax.numpy as jnp
from jax import lax
from jax.experimental import pallas as pl
from jax.experimental.pallas import tpu as pltpu
from jax.sharding import PartitionSpec as P

PANEL = 256
NPANEL = 2
BLOCK = 128
SLAB = 8
TILE = 256
DEPTH = 512
NT = (((1,), (1,)), ((), ()))


def dot_full(a, b):
    return lax.dot_general(
        a, b, NT, precision=lax.Precision.HIGHEST, preferred_element_type=jnp.float32
    )


def dot_once(a, b):
    return lax.dot_general(a, b, NT, preferred_element_type=jnp.float32)


def gram_product(a, b):
    rank = a.shape[1] // 2
    return dot_once(a[:, :rank], b[:, :rank]) * dot_once(a[:, rank:], b[:, rank:])


def pick_rows(table_ref, index_row):
    count = index_row.shape[1]
    depth = min(DEPTH, table_ref.shape[1])
    parts = []
    for first in range(0, count, BLOCK):
        wanted = jnp.broadcast_to(index_row[:, first : first + BLOCK], (BLOCK, BLOCK)).T
        wanted = jnp.concatenate([wanted] * (depth // BLOCK), axis=1)
        total = jnp.zeros((BLOCK, table_ref.shape[0]), jnp.float32)
        for start in range(0, table_ref.shape[1], depth):
            place = lax.broadcasted_iota(jnp.int32, (BLOCK, depth), 1) + start
            one_hot = jnp.where(wanted == place, 1.0, 0.0).astype(jnp.bfloat16)
            total += dot_once(one_hot, table_ref[:, start : start + depth])
        parts.append(total.astype(jnp.bfloat16))
    return jnp.concatenate(parts, axis=0)


def eliminate(block):
    size = block.shape[0]
    lane = lax.broadcasted_iota(jnp.int32, (SLAB, size), 1)
    sub = lax.broadcasted_iota(jnp.int32, (SLAB, size), 0)
    work = block
    upper, inverse = [], []
    for slab in range(size // SLAB):
        low = SLAB * slab
        height = work.shape[0]
        cols = [
            jnp.broadcast_to(work[:, low + c : low + c + 1], (height, size)) for c in range(SLAB)
        ]
        inside = (lane >= low) & (lane < low + SLAB)
        rows = [jnp.where(inside, jnp.where(lane - low == sub, 1.0, 0.0), work[:SLAB])]
        for first in range(SLAB, height, SLAB):
            rows.append(jnp.where(inside, 0.0, work[first : first + SLAB]))
        rows = jnp.concatenate(rows, axis=0)
        scale = jnp.zeros((SLAB, size), jnp.float32)
        diagonal = jnp.zeros((SLAB, size), jnp.float32)
        for j in range(SLAB):
            pivots = [
                jnp.broadcast_to(cols[c][j : j + 1], (SLAB, size)) if c >= j else None
                for c in range(SLAB)
            ]
            scale = jnp.where(sub == j, lax.rsqrt(pivots[j]), scale)
            for c in range(j, SLAB):
                diagonal = jnp.where((sub == j) & (lane == low + c), pivots[c], diagonal)
            if j == SLAB - 1 and height == SLAB:
                break
            inv = 1.0 / pivots[j]
            times = cols[j] * jnp.broadcast_to(inv[:1], (height, size))
            head = jnp.where(sub > j, times[:SLAB], 0.0)
            times = jnp.concatenate([head, times[SLAB:]], axis=0) if height > SLAB else head
            for c in range(j + 1, SLAB):
                cols[c] = cols[c] - times * jnp.broadcast_to(pivots[c][:1], (height, size))
            rows = rows - times * jnp.broadcast_to(rows[j : j + 1], (height, size))
        head = rows[:SLAB]
        upper.append(jnp.where(lane >= low + SLAB, head * scale, diagonal * scale))
        inverse.append(jnp.where(lane < low + SLAB, head * scale, 0.0))
        work = rows[SLAB:]
    upper = jnp.concatenate(upper, axis=0)
    row = lax.broadcasted_iota(jnp.int32, (size, size), 0)
    col = lax.broadcasted_iota(jnp.int32, (size, size), 1)
    return jnp.where(col >= row, upper, 0.0), jnp.concatenate(inverse, axis=0)


def prefix_kernel(table_ref, index_ref, picked_ref, lower_ref, inverse_ref, work_ref):
    size = lower_ref.shape[0]
    picked = pick_rows(table_ref, index_ref[...])
    picked_ref[...] = picked
    row = lax.broadcasted_iota(jnp.int32, (size, size), 0)
    col = lax.broadcasted_iota(jnp.int32, (size, size), 1)
    work_ref[...] = gram_product(picked, picked) + jnp.where(row == col, 1.0, 0.0)
    lower_ref[...] = jnp.zeros_like(lower_ref)
    for start in range(0, size, BLOCK):
        stop = start + BLOCK
        upper, inverse = eliminate(work_ref[start:stop, start:stop])
        lower_ref[start:stop, start:stop] = upper.T
        inverse_ref[start:stop, :] = inverse
        if stop < size:
            below = dot_full(work_ref[stop:, start:stop], inverse)
            lower_ref[stop:, start:stop] = below
            for first in range(stop, size, BLOCK):
                last = first + BLOCK
                work_ref[first:, first:last] = work_ref[first:, first:last] - dot_full(
                    below[first - stop :], below[first - stop : last - stop]
                )


def solve_rows(rows_schur, lower_ref, inverse_ref):
    size = lower_ref.shape[0]
    parts = [rows_schur[:, s : s + BLOCK] for s in range(0, size, BLOCK)]
    solved = []
    for k in range(size // BLOCK):
        start = k * BLOCK
        here = dot_full(parts[k], inverse_ref[start : start + BLOCK, :])
        solved.append(here)
        for j in range(k + 1, size // BLOCK):
            parts[j] = parts[j] - dot_full(
                here, lower_ref[j * BLOCK : (j + 1) * BLOCK, start : start + BLOCK]
            )
    return jnp.concatenate(solved, axis=1)


def tile_kernel(
    place_ref, table_ref, rows_ref, cols_ref, picked_ref, lower_ref, inverse_ref,
    out_ref, col_vecs_ref, col_solved_ref, shown_ref,
):
    size = lower_ref.shape[0]
    height, width = out_ref.shape
    step = pl.program_id(0)
    row_start = place_ref[0] + step * height
    col_start = place_ref[1]
    in_prefix = col_start < size

    @pl.when((step == 0) & jnp.logical_not(in_prefix))
    def _():
        vecs = pick_rows(table_ref, cols_ref[...])
        col_vecs_ref[...] = vecs
        col_solved_ref[...] = solve_rows(gram_product(vecs, picked_ref[...]), lower_ref, inverse_ref)

    vecs = pick_rows(table_ref, rows_ref[...])
    row = lax.broadcasted_iota(jnp.int32, (height, size), 0) + row_start
    col = lax.broadcasted_iota(jnp.int32, (height, size), 1)
    plain = gram_product(vecs, picked_ref[...]) + jnp.where(row == col, 1.0, 0.0)
    solved = solve_rows(plain, lower_ref, inverse_ref)

    @pl.when(in_prefix)
    def _():
        shown = jnp.where(
            row >= (col // PANEL) * PANEL, jnp.where(col > row, 0.0, solved), plain
        )
        shown_ref[...] = shown
        out_ref[...] = shown_ref[:, pl.ds(pl.multiple_of(col_start, BLOCK), width)]

    @pl.when(jnp.logical_not(in_prefix))
    def _():
        masked = jnp.where(row >= (col // PANEL + 1) * PANEL, solved, 0.0)
        row_here = lax.broadcasted_iota(jnp.int32, (height, width), 0) + row_start
        col_here = lax.broadcasted_iota(jnp.int32, (height, width), 1) + col_start
        schur = gram_product(vecs, col_vecs_ref[...]) + jnp.where(row_here == col_here, 1.0, 0.0)
        out_ref[...] = schur - dot_full(masked, col_solved_ref[...])


def body(outcome_vectors, u_factor, v_factor, outcome_index):
    cols_n = lax.axis_size("col")
    factors = jnp.concatenate([u_factor, v_factor], axis=0)
    partial_value = lax.dot_general(factors, outcome_vectors, NT, preferred_element_type=jnp.float32)
    width = partial_value.shape[0]
    pieces = partial_value.reshape(width, cols_n, -1)
    summed = lax.all_to_all(pieces, "col", 1, 0, tiled=False).sum(0).astype(jnp.bfloat16)
    spread = jnp.broadcast_to(summed[None], (cols_n,) + summed.shape)
    own_block = lax.all_to_all(spread, "col", 0, 0, tiled=False)
    own_block = jnp.swapaxes(own_block, 0, 1).reshape(width, -1)
    table = lax.all_gather(own_block, "row", axis=1, tiled=True)
    total = table.shape[1]
    row_height = total // lax.axis_size("row")
    col_width = total // cols_n
    prefix = NPANEL * PANEL
    row_start = lax.axis_index("row") * row_height
    col_start = lax.axis_index("col") * col_width
    index = outcome_index[None, :]
    row_ids = lax.dynamic_slice_in_dim(index, row_start, row_height, 1)
    col_ids = lax.dynamic_slice_in_dim(index, col_start, col_width, 1)
    grant = pltpu.CompilerParams(vmem_limit_bytes=48 * 2**20)
    picked, lower, inverse = pl.pallas_call(
        prefix_kernel,
        out_shape=(
            jax.ShapeDtypeStruct((prefix, width), jnp.bfloat16),
            jax.ShapeDtypeStruct((prefix, prefix), jnp.float32),
            jax.ShapeDtypeStruct((prefix, BLOCK), jnp.float32),
        ),
        scratch_shapes=[pltpu.VMEM((prefix, prefix), jnp.float32)],
        compiler_params=grant,
        name="prefix_factor",
    )(table, index[:, :prefix])
    place = jnp.stack([row_start, col_start]).astype(jnp.int32)
    whole = lambda a: pl.BlockSpec(a.shape, lambda i: (0,) * a.ndim)
    return pl.pallas_call(
        tile_kernel,
        grid=(row_height // TILE,),
        in_specs=[
            pl.BlockSpec(memory_space=pltpu.SMEM),
            whole(table),
            pl.BlockSpec((1, TILE), lambda i: (0, i)),
            whole(col_ids),
            whole(picked),
            whole(lower),
            whole(inverse),
        ],
        out_specs=pl.BlockSpec((TILE, col_width), lambda i: (i, 0)),
        out_shape=jax.ShapeDtypeStruct((row_height, col_width), jnp.float32),
        scratch_shapes=[
            pltpu.VMEM((col_width, width), jnp.bfloat16),
            pltpu.VMEM((col_width, prefix), jnp.float32),
            pltpu.VMEM((TILE, prefix), jnp.float32),
        ],
        compiler_params=grant,
        name="tile_update",
    )(place, table, row_ids, col_ids, picked, lower, inverse)


def solution(mesh):
    placed = (P("row", "col"), P(None, "col"), P(None, "col"), P())
    return jax.shard_map(
        body, mesh=mesh, in_specs=placed, out_specs=P("row", "col"), check_vma=False
    )
```

```python
import jax
import jax.numpy as jnp
from jax import lax
from jax.experimental import pallas as pl
from jax.experimental.pallas import tpu as pltpu
from jax.sharding import PartitionSpec as P

PANEL = 256
NPANEL = 2
BLOCK = 128
SLAB = 8
TILE = 256
DEPTH = 256
LANES = 128
NEAR = 4
TN = (((0,), (0,)), ((), ()))
NT = (((1,), (1,)), ((), ()))


def dot_full(a, b):
    return lax.dot_general(
        a, b, NT, precision=lax.Precision.HIGHEST, preferred_element_type=jnp.float32
    )


def dot_once(a, b):
    return lax.dot_general(a, b, NT, preferred_element_type=jnp.float32)


def gram_product(a, b):
    rank = a.shape[1] // 2
    return dot_once(a[:, :rank], b[:, :rank]) * dot_once(a[:, rank:], b[:, rank:])


def split_index(index_row):
    count = index_row.shape[1]
    parts = []
    for first in range(0, count, BLOCK):
        parts.append(jnp.broadcast_to(index_row[:, first : first + BLOCK], (BLOCK, BLOCK)).T)
    wanted = jnp.concatenate(parts, axis=0)
    return wanted % DEPTH, wanted // DEPTH


def pick_rows(table_ref, index_row):
    width, total = table_ref.shape
    within, run = split_index(index_row)
    place = lax.broadcasted_iota(jnp.int32, within.shape, 1)
    one_hot = jnp.concatenate(
        [jnp.where(within == place + s, 1.0, 0.0) for s in range(0, DEPTH, LANES)], axis=1
    ).astype(jnp.bfloat16)
    each = LANES // width
    runs_at_once = 2 * each
    picked = jnp.zeros(within.shape, jnp.float32)
    for first in range(0, total // DEPTH, runs_at_once):
        runs = jnp.concatenate(
            [table_ref[:, r * DEPTH : (r + 1) * DEPTH] for r in range(first, first + runs_at_once)],
            axis=0,
        )
        found = dot_once(one_hot, runs)
        for half in range(2):
            here = run == first + half * each + place // width
            picked = jnp.where(here, found[:, half * LANES : (half + 1) * LANES], picked)
    out = picked[:, :width]
    for s in range(width, LANES, width):
        out = out + picked[:, s : s + width]
    return out.astype(jnp.bfloat16)


def lanes(x, index):
    return jnp.take_along_axis(x, index, axis=1, mode="promise_in_bounds")


def split_three(x):
    high = x.astype(jnp.bfloat16).astype(jnp.float32)
    rest = x - high
    mid = rest.astype(jnp.bfloat16).astype(jnp.float32)
    return high, mid, rest - mid


def eliminate(block, near=NEAR):
    size = block.shape[0]
    tiles = size // LANES
    shape=(SLAB,LANES)
    lane = lax.broadcasted_iota(jnp.int32, shape, 1)
    sub = lax.broadcasted_iota(jnp.int32, shape, 0)
    work=[[block[s:s+SLAB,i*LANES:(i+1)*LANES] for i in range(tiles)] for s in range(0,size,SLAB)]
    upper, inverse = [], []
    for slab in range(size // SLAB):
        here, low = divmod(SLAB * slab, LANES)
        inside = (lane >= low) & (lane < low + SLAB)
        count=min(near,len(work))
        cols=[[None]*SLAB for _ in range(count)]
        for c in range(SLAB):
            pattern=jnp.full(shape, low + c, jnp.int32)
            for t in range(count): cols[t][c]=lanes(work[t][here],pattern)
        rows=[list(w) for w in work]
        rows[0][here]=jnp.where(inside, jnp.where(lane - low == sub, 1.0, 0.0), work[0][here])
        for t in range(1,len(work)): rows[t][here]=jnp.where(inside, 0.0, work[t][here])
        own = work[0][here]
        for j in range(SLAB):
            if j == SLAB - 1 and len(work) == 1:
                break
            pivots = [jnp.broadcast_to(cols[0][c][j : j + 1], shape) if c >= j else None for c in range(SLAB)]
            inv = 1.0 / pivots[j]
            top = [jnp.broadcast_to(r[j:j+1], shape) for r in rows[0]]
            top_own = jnp.broadcast_to(own[j:j+1], shape)
            for t in range(count):
                times = cols[t][j] * inv
                if t == 0: times = jnp.where(sub > j, times, 0.0)
                for c in range(j + 1, SLAB):
                    cols[t][c] = cols[t][c] - times * pivots[c]
                for i in range(tiles): rows[t][i] = rows[t][i] - times * top[i]
                if t == 0: own = own - times * top_own
        diagonal = lanes(own, low + sub)
        scale = lax.rsqrt(diagonal)
        factor=[jnp.zeros(shape,jnp.float32)]*here + [jnp.where(lane>=low+sub,own*scale,0.0)] + [r*scale for r in rows[0][here+1:]]
        back=[r*scale for r in rows[0][:here]] + [jnp.where(lane < low + SLAB, rows[0][here] * scale, 0.0)] + [jnp.zeros(shape,jnp.float32)]*(tiles-here-1)
        upper.append(jnp.concatenate(factor,1)); inverse.append(jnp.concatenate(back,1))
        if len(work)>count:
            tip=jnp.concatenate([r*scale for r in rows[0]],1)
            left=jnp.concatenate(factor,1)
            h, m, l = split_three(left)
            H, M, Lo = split_three(tip)
            a = jnp.concatenate([h, h, m, m, h, l], axis=0).astype(jnp.bfloat16)
            b = jnp.concatenate([H, M, H, M, Lo, H], axis=0).astype(jnp.bfloat16)
            start=SLAB*(slab+count)
            aligned=start//LANES*LANES
            update=lax.dot_general(a[:,aligned:],b,TN,preferred_element_type=jnp.float32)
            for t in range(count,len(work)):
                s=SLAB*(slab+t)-aligned
                for i in range(tiles): rows[t][i]=rows[t][i]-update[s:s+SLAB,i*LANES:(i+1)*LANES]
        work = rows[1:]
    join=lambda a: jnp.concatenate(a, axis=0)
    return join(upper), join(inverse)


def split_pair(x):
    high = x.astype(jnp.bfloat16)
    return high, (x - high.astype(jnp.float32)).astype(jnp.bfloat16)


def as_left(x):
    high, low = split_pair(x)
    return jnp.concatenate([high, high, low], axis=1)


def as_right(x):
    high, low = split_pair(x)
    return jnp.concatenate([high, low, high], axis=1)


def prefix_kernel(
    table_ref, index_ref, picked_ref, lower_ref, inverse_ref, work_ref
):
    size = work_ref.shape[0]
    picked = pick_rows(table_ref, index_ref[...])
    picked_ref[...] = picked
    row = lax.broadcasted_iota(jnp.int32, (size, size), 0)
    col = lax.broadcasted_iota(jnp.int32, (size, size), 1)
    work_ref[...] = gram_product(picked, picked) + jnp.where(row == col, 1.0, 0.0)
    for start in range(0, size, PANEL):
        stop = start + PANEL
        upper, inverse = eliminate(work_ref[start:stop, start:stop])
        inverse_ref[start:stop, :] = as_right(inverse)
        if stop < size:
            below = dot_full(work_ref[stop:, start:stop], inverse)
            work_ref[stop:, stop:] = work_ref[stop:, stop:] - dot_full(below, below)
            lower_ref[stop - PANEL : size - PANEL, start * 3 : stop * 3] = as_right(below)


def solve_rows(plain, lower_ref, inverse_ref):
    size = plain.shape[1]
    parts = [plain[:, s : s + PANEL] for s in range(0, size, PANEL)]
    solved = []
    for k in range(size // PANEL):
        start = k * PANEL
        here = dot_once(as_left(parts[k]), inverse_ref[start : start + PANEL, :])
        solved.append(here)
        for j in range(k + 1, size // PANEL):
            parts[j] = parts[j] - dot_once(
                as_left(here),
                lower_ref[(j - 1) * PANEL : j * PANEL, start * 3 : (start + PANEL) * 3],
            )
    return jnp.concatenate(solved, axis=1)


def tile_kernel(
    place_ref, table_ref, rows_ref, cols_ref, picked_ref, lower_ref, inverse_ref,
    out_ref, col_vecs_ref, col_solved_ref, shown_ref,
):
    size = picked_ref.shape[0]
    height, width = out_ref.shape
    step = pl.program_id(0)
    row_start = place_ref[0] + step * height
    col_start = place_ref[1]
    in_prefix = col_start < size

    @pl.when((step == 0) & jnp.logical_not(in_prefix))
    def _():
        vecs = pick_rows(table_ref, cols_ref[...])
        col_vecs_ref[...] = vecs
        col_solved_ref[...] = as_right(
            solve_rows(gram_product(vecs, picked_ref[...]), lower_ref, inverse_ref)
        )

    vecs = pick_rows(table_ref, rows_ref[...])
    row = lax.broadcasted_iota(jnp.int32, (height, size), 0) + row_start
    col = lax.broadcasted_iota(jnp.int32, (height, size), 1)
    plain = gram_product(vecs, picked_ref[...]) + jnp.where(row == col, 1.0, 0.0)
    solved = solve_rows(plain, lower_ref, inverse_ref)

    @pl.when(in_prefix)
    def _():
        shown_ref[...] = jnp.where(
            row >= (col // PANEL) * PANEL, jnp.where(col > row, 0.0, solved), plain
        )
        out_ref[...] = shown_ref[:, pl.ds(pl.multiple_of(col_start, BLOCK), width)]

    @pl.when(jnp.logical_not(in_prefix))
    def _():
        masked = jnp.where(row >= (col // PANEL + 1) * PANEL, solved, 0.0)
        row_here = lax.broadcasted_iota(jnp.int32, (height, width), 0) + row_start
        col_here = lax.broadcasted_iota(jnp.int32, (height, width), 1) + col_start
        schur = gram_product(vecs, col_vecs_ref[...]) + jnp.where(row_here == col_here, 1.0, 0.0)
        out_ref[...] = schur - dot_once(as_left(masked), col_solved_ref[...])


def body(outcome_vectors, u_factor, v_factor, outcome_index):
    cols_n = lax.axis_size("col")
    factors = jnp.concatenate([u_factor, v_factor], axis=0)
    partial_value = lax.dot_general(factors, outcome_vectors, NT, preferred_element_type=jnp.float32)
    width = partial_value.shape[0]
    pieces = partial_value.reshape(width, cols_n, -1)
    summed = lax.all_to_all(pieces, "col", 1, 0, tiled=False).sum(0).astype(jnp.bfloat16)
    spread = jnp.broadcast_to(summed[None], (cols_n,) + summed.shape)
    own_block = lax.all_to_all(spread, "col", 0, 0, tiled=False)
    own_block = jnp.swapaxes(own_block, 0, 1).reshape(width, -1)
    table = lax.all_gather(own_block, "row", axis=1, tiled=True)
    total = table.shape[1]
    row_height = total // lax.axis_size("row")
    col_width = total // cols_n
    prefix = NPANEL * PANEL
    row_start = lax.axis_index("row") * row_height
    col_start = lax.axis_index("col") * col_width
    index = outcome_index[None, :]
    row_ids = lax.dynamic_slice_in_dim(index, row_start, row_height, 1)
    col_ids = lax.dynamic_slice_in_dim(index, col_start, col_width, 1)
    grant = pltpu.CompilerParams(vmem_limit_bytes=48 * 2**20)
    picked, lower, inverse = pl.pallas_call(
        prefix_kernel,
        out_shape=(
            jax.ShapeDtypeStruct((prefix, width), jnp.bfloat16),
            jax.ShapeDtypeStruct((prefix - PANEL, 3 * (prefix - PANEL)), jnp.bfloat16),
            jax.ShapeDtypeStruct((prefix, 3 * PANEL), jnp.bfloat16),
        ),
        scratch_shapes=[pltpu.VMEM((prefix, prefix), jnp.float32)],
        compiler_params=grant,
        name="prefix_factor",
    )(table, index[:, :prefix])
    place = jnp.stack([row_start, col_start]).astype(jnp.int32)
    whole = lambda a: pl.BlockSpec(a.shape, lambda i: (0,) * a.ndim)
    return pl.pallas_call(
        tile_kernel,
        grid=(row_height // TILE,),
        in_specs=[
            pl.BlockSpec(memory_space=pltpu.SMEM),
            whole(table),
            pl.BlockSpec((1, TILE), lambda i: (0, i)),
            whole(col_ids),
            whole(picked),
            whole(lower),
            whole(inverse),
        ],
        out_specs=pl.BlockSpec((TILE, col_width), lambda i: (i, 0)),
        out_shape=jax.ShapeDtypeStruct((row_height, col_width), jnp.float32),
        scratch_shapes=[
            pltpu.VMEM((col_width, width), jnp.bfloat16),
            pltpu.VMEM((col_width, 3 * prefix), jnp.bfloat16),
            pltpu.VMEM((TILE, prefix), jnp.float32),
        ],
        compiler_params=grant,
        name="tile_update",
    )(place, table, row_ids, col_ids, picked, lower, inverse)


def solution(mesh):
    placed = (P("row", "col"), P(None, "col"), P(None, "col"), P())
    return jax.shard_map(
        body, mesh=mesh, in_specs=placed, out_specs=P("row", "col"), check_vma=False
    )
```

```python
import math

import jax
import jax.numpy as jnp
from jax import lax
from jax.experimental import pallas as pl
from jax.experimental.pallas import tpu as pltpu
from jax.sharding import PartitionSpec as P

PANEL = 256
NPANEL = 2
BLOCK = 128
SLAB = 8
TILE = 1024
DEPTH = 256
LANES = 128
NEAR = 4
TN = (((0,), (0,)), ((), ()))
LARGEST_VECTOR = 6.0
LARGEST_FACTOR = 0.03125
HALF_MAX = 65504.0
NT = (((1,), (1,)), ((), ()))


def dot_full(a, b):
    return lax.dot_general(
        a, b, NT, precision=lax.Precision.HIGHEST, preferred_element_type=jnp.float32
    )


def dot_once(a, b):
    return lax.dot_general(a, b, NT, preferred_element_type=jnp.float32)


def gram_product(a, b):
    rank = a.shape[1] // 2
    return dot_once(a[:, :rank], b[:, :rank]) * dot_once(a[:, rank:], b[:, rank:])


def split_index(index_row):
    count = index_row.shape[1]
    parts = []
    for first in range(0, count, BLOCK):
        parts.append(jnp.broadcast_to(index_row[:, first : first + BLOCK], (BLOCK, BLOCK)).T)
    wanted = jnp.concatenate(parts, axis=0)
    return wanted % DEPTH, wanted // DEPTH


def pick_rows(table_ref, index_row):
    width, total = table_ref.shape
    within, run = split_index(index_row)
    place = lax.broadcasted_iota(jnp.int32, within.shape, 1)
    one_hot = jnp.concatenate(
        [jnp.where(within == place + s, 1.0, 0.0) for s in range(0, DEPTH, LANES)], axis=1
    ).astype(jnp.bfloat16)
    each = LANES // width
    runs_at_once = 2 * each
    picked = jnp.zeros(within.shape, jnp.float32)
    for first in range(0, total // DEPTH, runs_at_once):
        runs = jnp.concatenate(
            [table_ref[:, r * DEPTH : (r + 1) * DEPTH] for r in range(first, first + runs_at_once)],
            axis=0,
        )
        found = dot_once(one_hot, runs)
        for half in range(2):
            here = run == first + half * each + place // width
            picked = jnp.where(here, found[:, half * LANES : (half + 1) * LANES], picked)
    out = picked[:, :width]
    for s in range(width, LANES, width):
        out = out + picked[:, s : s + width]
    return out.astype(jnp.bfloat16)


def lanes(x, index):
    return jnp.take_along_axis(x, index, axis=1, mode="promise_in_bounds")


def split_three(x):
    high = x.astype(jnp.bfloat16).astype(jnp.float32)
    rest = x - high
    mid = rest.astype(jnp.bfloat16).astype(jnp.float32)
    return high, mid, rest - mid


def eliminate(block, near=NEAR):
    size = block.shape[0]
    tiles = size // LANES
    shape=(SLAB,LANES)
    lane = lax.broadcasted_iota(jnp.int32, shape, 1)
    sub = lax.broadcasted_iota(jnp.int32, shape, 0)
    work=[[block[s:s+SLAB,i*LANES:(i+1)*LANES] for i in range(tiles)] for s in range(0,size,SLAB)]
    upper, inverse = [], []
    for slab in range(size // SLAB):
        here, low = divmod(SLAB * slab, LANES)
        inside = (lane >= low) & (lane < low + SLAB)
        count=min(near,len(work))
        cols=[[None]*SLAB for _ in range(count)]
        for c in range(SLAB):
            pattern=jnp.full(shape, low + c, jnp.int32)
            for t in range(count): cols[t][c]=lanes(work[t][here],pattern)
        rows=[list(w) for w in work]
        rows[0][here]=jnp.where(inside, jnp.where(lane - low == sub, 1.0, 0.0), work[0][here])
        for t in range(1,len(work)): rows[t][here]=jnp.where(inside, 0.0, work[t][here])
        own = work[0][here]
        for j in range(SLAB):
            if j == SLAB - 1 and len(work) == 1:
                break
            pivots = [jnp.broadcast_to(cols[0][c][j : j + 1], shape) if c >= j else None for c in range(SLAB)]
            inv = 1.0 / pivots[j]
            top = [jnp.broadcast_to(r[j:j+1], shape) for r in rows[0]]
            top_own = jnp.broadcast_to(own[j:j+1], shape)
            for t in range(count):
                times = cols[t][j] * inv
                if t == 0: times = jnp.where(sub > j, times, 0.0)
                for c in range(j + 1, SLAB):
                    cols[t][c] = cols[t][c] - times * pivots[c]
                for i in range(tiles): rows[t][i] = rows[t][i] - times * top[i]
                if t == 0: own = own - times * top_own
        diagonal = lanes(own, low + sub)
        scale = lax.rsqrt(diagonal)
        factor=[jnp.zeros(shape,jnp.float32)]*here + [jnp.where(lane>=low+sub,own*scale,0.0)] + [r*scale for r in rows[0][here+1:]]
        back=[r*scale for r in rows[0][:here]] + [jnp.where(lane < low + SLAB, rows[0][here] * scale, 0.0)] + [jnp.zeros(shape,jnp.float32)]*(tiles-here-1)
        upper.append(jnp.concatenate(factor,1)); inverse.append(jnp.concatenate(back,1))
        if len(work)>count:
            tip=jnp.concatenate([r*scale for r in rows[0]],1)
            left=jnp.concatenate(factor,1)
            h, m, l = split_three(left)
            H, M, Lo = split_three(tip)
            a = jnp.concatenate([h, h, m, m, h, l], axis=0).astype(jnp.bfloat16)
            b = jnp.concatenate([H, M, H, M, Lo, H], axis=0).astype(jnp.bfloat16)
            start=SLAB*(slab+count)
            aligned=start//LANES*LANES
            update=lax.dot_general(a[:,aligned:],b,TN,preferred_element_type=jnp.float32)
            for t in range(count,len(work)):
                s=SLAB*(slab+t)-aligned
                for i in range(tiles): rows[t][i]=rows[t][i]-update[s:s+SLAB,i*LANES:(i+1)*LANES]
        work = rows[1:]
    join=lambda a: jnp.concatenate(a, axis=0)
    return join(upper), join(inverse)


def split_pair(x):
    high = x.astype(jnp.bfloat16)
    return high, (x - high.astype(jnp.float32)).astype(jnp.bfloat16)


def as_left(x):
    high, low = split_pair(x)
    return jnp.concatenate([high, high, low], axis=1)


def as_right(x):
    high, low = split_pair(x)
    return jnp.concatenate([high, low, high], axis=1)


def prefix_kernel(
    table_ref, index_ref, picked_ref, lower_ref, inverse_ref, work_ref
):
    size = work_ref.shape[0]
    picked = pick_rows(table_ref, index_ref[...])
    picked_ref[...] = picked
    row = lax.broadcasted_iota(jnp.int32, (size, size), 0)
    col = lax.broadcasted_iota(jnp.int32, (size, size), 1)
    work_ref[...] = gram_product(picked, picked) + jnp.where(row == col, 1.0, 0.0)
    for start in range(0, size, PANEL):
        stop = start + PANEL
        upper, inverse = eliminate(work_ref[start:stop, start:stop])
        inverse_ref[start:stop, :] = as_right(inverse)
        if stop < size:
            below = dot_full(work_ref[stop:, start:stop], inverse)
            work_ref[stop:, stop:] = work_ref[stop:, stop:] - dot_full(below, below)
            lower_ref[stop - PANEL : size - PANEL, start * 3 : stop * 3] = as_right(below)


def solve_rows(plain, lower_ref, inverse_ref):
    size = plain.shape[1]
    parts = [plain[:, s : s + PANEL] for s in range(0, size, PANEL)]
    solved = []
    for k in range(size // PANEL):
        start = k * PANEL
        here = dot_once(as_left(parts[k]), inverse_ref[start : start + PANEL, :])
        solved.append(here)
        for j in range(k + 1, size // PANEL):
            parts[j] = parts[j] - dot_once(
                as_left(here),
                lower_ref[(j - 1) * PANEL : j * PANEL, start * 3 : (start + PANEL) * 3],
            )
    return jnp.concatenate(solved, axis=1)


def tile_kernel(
    place_ref, table_ref, rows_ref, cols_ref, picked_ref, lower_ref, inverse_ref,
    out_ref, col_vecs_ref, col_solved_ref, shown_ref,
):
    size = picked_ref.shape[0]
    height, width = out_ref.shape
    step = pl.program_id(0)
    row_start = place_ref[0] + step * height
    col_start = place_ref[1]
    in_prefix = col_start < size

    @pl.when((step == 0) & jnp.logical_not(in_prefix))
    def _():
        vecs = pick_rows(table_ref, cols_ref[...])
        col_vecs_ref[...] = vecs
        col_solved_ref[...] = as_right(
            solve_rows(gram_product(vecs, picked_ref[...]), lower_ref, inverse_ref)
        )

    vecs = pick_rows(table_ref, rows_ref[...])
    row = lax.broadcasted_iota(jnp.int32, (height, size), 0) + row_start
    col = lax.broadcasted_iota(jnp.int32, (height, size), 1)
    plain = gram_product(vecs, picked_ref[...]) + jnp.where(row == col, 1.0, 0.0)
    solved = solve_rows(plain, lower_ref, inverse_ref)

    @pl.when(in_prefix)
    def _():
        shown_ref[...] = jnp.where(
            row >= (col // PANEL) * PANEL, jnp.where(col > row, 0.0, solved), plain
        )
        out_ref[...] = shown_ref[:, pl.ds(pl.multiple_of(col_start, BLOCK), width)]

    @pl.when(jnp.logical_not(in_prefix))
    def _():
        masked = jnp.where(row >= (col // PANEL + 1) * PANEL, solved, 0.0)
        row_here = lax.broadcasted_iota(jnp.int32, (height, width), 0) + row_start
        col_here = lax.broadcasted_iota(jnp.int32, (height, width), 1) + col_start
        schur = gram_product(vecs, col_vecs_ref[...]) + jnp.where(row_here == col_here, 1.0, 0.0)
        out_ref[...] = schur - dot_once(as_left(masked), col_solved_ref[...])


def sum_over(value, axis, depth):
    size = lax.axis_size(axis)
    bound = LARGEST_VECTOR * LARGEST_FACTOR * depth
    scale = 2.0 ** math.floor(math.log2(HALF_MAX / bound))
    value = value * scale
    step = 1
    while step < size:
        sent = lax.reduce_precision(value, 5, 10)
        pairs = [(i, i ^ step) for i in range(size)]
        value = sent + lax.ppermute(sent.astype(jnp.float16), axis, pairs).astype(jnp.float32)
        step *= 2
    return value * (1.0 / scale)


def body(outcome_vectors, u_factor, v_factor, outcome_index):
    cols_n = lax.axis_size("col")
    factors = jnp.concatenate([u_factor, v_factor], axis=0)
    partial_value = lax.dot_general(factors, outcome_vectors, NT, preferred_element_type=jnp.float32)
    width = partial_value.shape[0]
    own_block = sum_over(partial_value, "col", outcome_vectors.shape[1] * cols_n)
    table = lax.all_gather(own_block.astype(jnp.bfloat16), "row", axis=1, tiled=True)
    total = table.shape[1]
    row_height = total // lax.axis_size("row")
    col_width = total // cols_n
    prefix = NPANEL * PANEL
    row_start = lax.axis_index("row") * row_height
    col_start = lax.axis_index("col") * col_width
    index = outcome_index[None, :]
    row_ids = lax.dynamic_slice_in_dim(index, row_start, row_height, 1)
    col_ids = lax.dynamic_slice_in_dim(index, col_start, col_width, 1)
    grant = pltpu.CompilerParams(vmem_limit_bytes=48 * 2**20)
    picked, lower, inverse = pl.pallas_call(
        prefix_kernel,
        out_shape=(
            jax.ShapeDtypeStruct((prefix, width), jnp.bfloat16),
            jax.ShapeDtypeStruct((prefix - PANEL, 3 * (prefix - PANEL)), jnp.bfloat16),
            jax.ShapeDtypeStruct((prefix, 3 * PANEL), jnp.bfloat16),
        ),
        scratch_shapes=[pltpu.VMEM((prefix, prefix), jnp.float32)],
        compiler_params=grant,
        name="prefix_factor",
    )(table, index[:, :prefix])
    place = jnp.stack([row_start, col_start]).astype(jnp.int32)
    whole = lambda a: pl.BlockSpec(a.shape, lambda i: (0,) * a.ndim)
    return pl.pallas_call(
        tile_kernel,
        grid=(row_height // TILE,),
        in_specs=[
            pl.BlockSpec(memory_space=pltpu.SMEM),
            whole(table),
            pl.BlockSpec((1, TILE), lambda i: (0, i)),
            whole(col_ids),
            whole(picked),
            whole(lower),
            whole(inverse),
        ],
        out_specs=pl.BlockSpec((TILE, col_width), lambda i: (i, 0)),
        out_shape=jax.ShapeDtypeStruct((row_height, col_width), jnp.float32),
        scratch_shapes=[
            pltpu.VMEM((col_width, width), jnp.bfloat16),
            pltpu.VMEM((col_width, 3 * prefix), jnp.bfloat16),
            pltpu.VMEM((TILE, prefix), jnp.float32),
        ],
        compiler_params=grant,
        name="tile_update",
    )(place, table, row_ids, col_ids, picked, lower, inverse)


def solution(mesh):
    placed = (P("row", "col"), P(None, "col"), P(None, "col"), P())
    return jax.shard_map(
        body, mesh=mesh, in_specs=placed, out_specs=P("row", "col"), check_vma=False
    )
```

```python
import functools
import math

import jax
import jax.numpy as jnp
from jax import lax
from jax.experimental import pallas as pl
from jax.experimental.pallas import tpu as pltpu
from jax.sharding import PartitionSpec as P

PANEL = 256
NPANEL = 2
BLOCK = 128
SLAB = 8
CHUNK = 256
DEPTH = 256
LANES = 128
NEAR = 4
TN = (((0,), (0,)), ((), ()))
LARGEST_VECTOR = 6.0
LARGEST_FACTOR = 0.03125
HALF_MAX = 65504.0
NT = (((1,), (1,)), ((), ()))


def dot_full(a, b):
    return lax.dot_general(
        a, b, NT, precision=lax.Precision.HIGHEST, preferred_element_type=jnp.float32
    )


def dot_once(a, b):
    return lax.dot_general(a, b, NT, preferred_element_type=jnp.float32)


def gram_product(a, b):
    rank = a.shape[1] // 2
    return dot_once(a[:, :rank], b[:, :rank]) * dot_once(a[:, rank:], b[:, rank:])


def split_index(index_row):
    count = index_row.shape[1]
    parts = []
    for first in range(0, count, BLOCK):
        parts.append(jnp.broadcast_to(index_row[:, first : first + BLOCK], (BLOCK, BLOCK)).T)
    wanted = jnp.concatenate(parts, axis=0)
    return wanted % DEPTH, wanted // DEPTH


def pick_rows(table_ref, index_row):
    width, total = table_ref.shape
    within, run = split_index(index_row)
    place = lax.broadcasted_iota(jnp.int32, within.shape, 1)
    one_hot = jnp.concatenate(
        [jnp.where(within == place + s, 1.0, 0.0) for s in range(0, DEPTH, LANES)], axis=1
    ).astype(jnp.bfloat16)
    each = LANES // width
    runs_at_once = 2 * each
    picked = jnp.zeros(within.shape, jnp.float32)
    for first in range(0, total // DEPTH, runs_at_once):
        runs = jnp.concatenate(
            [table_ref[:, r * DEPTH : (r + 1) * DEPTH] for r in range(first, first + runs_at_once)],
            axis=0,
        )
        found = dot_once(one_hot, runs)
        for half in range(2):
            here = run == first + half * each + place // width
            picked = jnp.where(here, found[:, half * LANES : (half + 1) * LANES], picked)
    out = picked[:, :width]
    for s in range(width, LANES, width):
        out = out + picked[:, s : s + width]
    return out.astype(jnp.bfloat16)


def lanes(x, index):
    return jnp.take_along_axis(x, index, axis=1, mode="promise_in_bounds")


def split_three(x):
    high = x.astype(jnp.bfloat16).astype(jnp.float32)
    rest = x - high
    mid = rest.astype(jnp.bfloat16).astype(jnp.float32)
    return high, mid, rest - mid


def eliminate(block, side):
    size = block.shape[0]
    tiles = size // LANES
    shape = (SLAB, LANES)
    lane = lax.broadcasted_iota(jnp.int32, shape, 1)
    sub = lax.broadcasted_iota(jnp.int32, shape, 0)
    zero = jnp.zeros(shape, jnp.float32)
    work = [
        [block[s : s + SLAB, i * LANES : (i + 1) * LANES] for i in range(tiles)]
        for s in range(0, size, SLAB)
    ]
    upper, inverse = [], []

    def column(slab_rows, at):
        return lanes(slab_rows[at // LANES], jnp.full(shape, at % LANES, jnp.int32))

    def spread(x, r):
        return jnp.broadcast_to(x[r : r + 1], shape)

    for slab in range(size // SLAB):
        at = SLAB * slab
        here, low = divmod(at, LANES)
        inside = (lane >= low) & (lane < low + SLAB)
        count = min(NEAR, len(work))
        cols = [[column(w, at + c) for c in range(SLAB)] for w in work[:count]]
        rows = [list(w) for w in work]
        rows[0][here] = jnp.where(inside, jnp.where(lane - low == sub, 1.0, 0.0), work[0][here])
        for t in range(1, len(work)):
            rows[t][here] = jnp.where(inside, 0.0, work[t][here])
        own = work[0][here]
        pivot = spread(cols[0][0], 0)
        scale = pivot
        for j in range(SLAB):
            if j == SLAB - 1 and len(work) == 1:
                break
            inv = 1.0 / pivot
            pivots = [spread(cols[0][c], j) if c > j else None for c in range(SLAB)]
            if j + 1 < SLAB:
                next_pivot = spread(cols[0][j + 1], j + 1) - pivots[j + 1] * pivots[j + 1] * inv
            top = [spread(r, j) for r in rows[0]]
            top_own = spread(own, j)
            for t in range(count):
                times = cols[t][j] * inv
                if t == 0:
                    times = jnp.where(sub > j, times, 0.0)
                    own = own - times * top_own
                for c in range(j + 1, SLAB):
                    cols[t][c] = cols[t][c] - times * pivots[c]
                for i in range(tiles):
                    rows[t][i] = rows[t][i] - times * top[i]
            if j + 1 < SLAB:
                pivot = next_pivot
                scale = jnp.where(sub >= j + 1, pivot, scale)
        scale = lax.rsqrt(scale)
        factor = [zero] * here + [jnp.where(lane >= low + sub, own * scale, 0.0)]
        factor += [r * scale for r in rows[0][here + 1 :]]
        back = [r * scale for r in rows[0][:here]]
        back += [jnp.where(lane < low + SLAB, rows[0][here] * scale, 0.0)] + [zero] * (tiles - here - 1)
        upper.append(jnp.concatenate(factor, axis=1))
        inverse.append(jnp.concatenate(back, axis=1))
        if len(work) > count:
            h, m, l = split_three(jnp.concatenate(factor, axis=1))
            H, M, Lo = split_three(jnp.concatenate([r * scale for r in rows[0]], axis=1))
            left = jnp.concatenate([h, h, m, m, h, l], axis=0).astype(jnp.bfloat16)
            right = jnp.concatenate([H, M, H, M, Lo, H], axis=0).astype(jnp.bfloat16)
            aligned = SLAB * (slab + count) // LANES * LANES
            update = lax.dot_general(
                left[:, aligned:], right, TN, preferred_element_type=jnp.float32
            )
            for t in range(count, len(work)):
                first = SLAB * (slab + t) - aligned
                for i in range(tiles):
                    rows[t][i] = rows[t][i] - update[first : first + SLAB, i * LANES : (i + 1) * LANES]
        work = rows[1:]
        side()
    return jnp.concatenate(upper, axis=0), jnp.concatenate(inverse, axis=0)


def split_pair(x):
    high = x.astype(jnp.bfloat16)
    return high, (x - high.astype(jnp.float32)).astype(jnp.bfloat16)


def as_left(x):
    high, low = split_pair(x)
    return jnp.concatenate([high, high, low], axis=1)


def as_right(x):
    high, low = split_pair(x)
    return jnp.concatenate([high, low, high], axis=1)


def tile_kernel(
    place_ref, table_ref, first_ref, rows_ref, cols_ref, out_ref,
    lead_ref, vecs_ref, plain_ref, left_ref, right_ref, rest_ref, work_ref, back_ref, lower_ref, shown_ref,
):
    height, width = out_ref.shape
    size = work_ref.shape[0]
    steps = size // PANEL
    row_start = place_ref[0]
    col_start = place_ref[1]
    col_chunks = [(s, min(CHUNK, width - s)) for s in range(0, width, CHUNK)]
    row_chunks = [(width + s, min(CHUNK, height - s)) for s in range(0, height, CHUNK)]

    def numbers(start, count, across):
        first = row_start + (start - width) if start >= width else col_start + start
        return lax.broadcasted_iota(jnp.int32, (count, across), 0) + first

    def gather(start, count):
        index = cols_ref[:, start : start + count] if start < width else rows_ref[
            :, start - width : start - width + count
        ]
        vecs = pick_rows(table_ref, index)
        vecs_ref[start : start + count, :] = vecs

    def plain(start, count, panel):
        columns = slice(panel * PANEL, (panel + 1) * PANEL)
        row = numbers(start, count, PANEL)
        col = lax.broadcasted_iota(jnp.int32, (count, PANEL), 1) + panel * PANEL
        plain_ref[start : start + count, columns] = gram_product(
            vecs_ref[start : start + count, :], lead_ref[columns, :]
        ) + jnp.where(row == col, 1.0, 0.0)

    def schur(start, count):
        row = numbers(start, count, width)
        col = lax.broadcasted_iota(jnp.int32, (count, width), 1) + col_start
        out_ref[start - width : start - width + count, :] = gram_product(
            vecs_ref[start : start + count, :], vecs_ref[:width, :]
        ) + jnp.where(row == col, 1.0, 0.0)

    def solve(start, count, panel):
        here = slice(start, start + count)
        columns = slice(panel * PANEL, (panel + 1) * PANEL)
        source = plain_ref if panel == 0 else rest_ref
        found = dot_once(as_left(source[here, columns]), back_ref[columns, :])
        if start < width:
            right_ref[here, panel * 3 * PANEL : (panel + 1) * 3 * PANEL] = as_right(found)
        else:
            row = numbers(start, count, PANEL)
            at = slice(start - width, start - width + count)
            masked = jnp.where(row >= (panel + 1) * PANEL, found, 0.0)
            left_ref[at, panel * 3 * PANEL : (panel + 1) * 3 * PANEL] = as_left(masked)
            col = lax.broadcasted_iota(jnp.int32, (count, PANEL), 1) + panel * PANEL
            shown = jnp.where(
                row >= panel * PANEL, jnp.where(col > row, 0.0, found), plain_ref[here, columns]
            )
            shown_ref[at, columns] = shown
        for later in range(panel + 1, steps):
            onward = slice(later * PANEL, (later + 1) * PANEL)
            source = plain_ref if panel == 0 else rest_ref
            rest_ref[here, onward] = source[here, onward] - dot_once(
                as_left(found),
                lower_ref[onward, panel * 3 * PANEL : (panel + 1) * 3 * PANEL],
            )

    def update(start, count, panel):
        at = slice(start - width, start - width + count)
        columns = slice(panel * 3 * PANEL, (panel + 1) * 3 * PANEL)
        out_ref[at, :] = out_ref[at, :] - dot_once(left_ref[at, columns], right_ref[:, columns])

    def lead_rows(panel):
        columns = slice(panel * PANEL, (panel + 1) * PANEL)
        lead_ref[columns, :] = pick_rows(table_ref, first_ref[:, columns])

    def lead_block(row_panel, col_panel):
        rows = slice(row_panel * PANEL, (row_panel + 1) * PANEL)
        columns = slice(col_panel * PANEL, (col_panel + 1) * PANEL)
        row = lax.broadcasted_iota(jnp.int32, (PANEL, PANEL), 0) + row_panel * PANEL
        col = lax.broadcasted_iota(jnp.int32, (PANEL, PANEL), 1) + col_panel * PANEL
        work_ref[rows, columns] = gram_product(lead_ref[rows, :], lead_ref[columns, :]) + jnp.where(
            row == col, 1.0, 0.0
        )

    both = col_chunks + row_chunks
    early = []
    for p in range(1, steps):
        early.append(functools.partial(lead_rows, p))
        for q in range(p + 1):
            early.append(functools.partial(lead_block, p, q))
    for chunk in both:
        early.append(functools.partial(gather, *chunk))
        early += [functools.partial(plain, *chunk, p) for p in range(steps)]
    early += [functools.partial(schur, *chunk) for chunk in row_chunks]
    tasks = []
    for p in range(steps):
        if p == 0:
            tasks.append(early)
        else:
            tasks.append(
                [functools.partial(solve, *chunk, p - 1) for chunk in both]
                + [functools.partial(update, *chunk, p - 1) for chunk in row_chunks]
            )

    lead_rows(0)
    lead_block(0, 0)
    for p in range(steps):
        start, stop = p * PANEL, (p + 1) * PANEL
        todo = tasks[p]
        done = [0, 0]

        def side():
            done[0] += 1
            target = -(-len(todo) * done[0] // (PANEL // SLAB))
            while done[1] < target:
                todo[done[1]]()
                done[1] += 1

        upper, inverse = eliminate(work_ref[start:stop, start:stop], side)
        back_ref[start:stop, :] = as_right(inverse)
        for q in range(p + 1, steps):
            rows = slice(q * PANEL, (q + 1) * PANEL)
            below = dot_full(work_ref[rows, start:stop], inverse)
            lower_ref[rows, start * 3 : stop * 3] = as_right(below)
            for r in range(p + 1, q + 1):
                columns = slice(r * PANEL, (r + 1) * PANEL)
                other = below if r == q else dot_full(work_ref[columns, start:stop], inverse)
                work_ref[rows, columns] = work_ref[rows, columns] - dot_full(below, other)
    for chunk in both:
        solve(*chunk, steps - 1)
    in_prefix = col_start < size

    @pl.when(in_prefix)
    def _():
        out_ref[...] = shown_ref[:, pl.ds(pl.multiple_of(col_start, LANES), width)]

    @pl.when(jnp.logical_not(in_prefix))
    def _():
        for chunk in row_chunks:
            update(*chunk, steps - 1)


def sum_over(value, axis, depth):
    size = lax.axis_size(axis)
    bound = LARGEST_VECTOR * LARGEST_FACTOR * depth
    scale = 2.0 ** math.floor(math.log2(HALF_MAX / bound))
    value = value * scale
    step = 1
    while step < size:
        sent = lax.reduce_precision(value, 5, 10)
        pairs = [(i, i ^ step) for i in range(size)]
        value = sent + lax.ppermute(sent.astype(jnp.float16), axis, pairs).astype(jnp.float32)
        step *= 2
    return value * (1.0 / scale)


def body(outcome_vectors, u_factor, v_factor, outcome_index):
    cols_n = lax.axis_size("col")
    factors = jnp.concatenate([u_factor, v_factor], axis=0)
    partial_value = lax.dot_general(factors, outcome_vectors, NT, preferred_element_type=jnp.float32)
    width = partial_value.shape[0]
    own_block = sum_over(partial_value, "col", outcome_vectors.shape[1] * cols_n)
    table = lax.all_gather(own_block.astype(jnp.bfloat16), "row", axis=1, tiled=True)
    total = table.shape[1]
    row_height = total // lax.axis_size("row")
    col_width = total // cols_n
    prefix = NPANEL * PANEL
    row_start = lax.axis_index("row") * row_height
    col_start = lax.axis_index("col") * col_width
    index = outcome_index[None, :]
    row_ids = lax.dynamic_slice_in_dim(index, row_start, row_height, 1)
    col_ids = lax.dynamic_slice_in_dim(index, col_start, col_width, 1)
    place = jnp.stack([row_start, col_start]).astype(jnp.int32)
    stack = row_height + col_width
    in_vmem = pl.BlockSpec(memory_space=pltpu.VMEM)
    return pl.pallas_call(
        tile_kernel,
        in_specs=[pl.BlockSpec(memory_space=pltpu.SMEM)] + [in_vmem] * 4,
        out_specs=in_vmem,
        out_shape=jax.ShapeDtypeStruct((row_height, col_width), jnp.float32),
        scratch_shapes=[
            pltpu.VMEM((prefix, width), jnp.bfloat16),
            pltpu.VMEM((stack, width), jnp.bfloat16),
            pltpu.VMEM((stack, prefix), jnp.float32),
            pltpu.VMEM((row_height, 3 * prefix), jnp.bfloat16),
            pltpu.VMEM((col_width, 3 * prefix), jnp.bfloat16),
            pltpu.VMEM((stack, prefix), jnp.float32),
            pltpu.VMEM((prefix, prefix), jnp.float32),
            pltpu.VMEM((prefix, 3 * PANEL), jnp.bfloat16),
            pltpu.VMEM((prefix, 3 * prefix), jnp.bfloat16),
            pltpu.VMEM((row_height, prefix), jnp.float32),
        ],
        compiler_params=pltpu.CompilerParams(vmem_limit_bytes=56 * 2**20),
        name="factor_and_update",
    )(place, table, index[:, :prefix], row_ids, col_ids)


def solution(mesh):
    placed = (P("row", "col"), P(None, "col"), P(None, "col"), P())
    return jax.shard_map(
        body, mesh=mesh, in_specs=placed, out_specs=P("row", "col"), check_vma=False
    )
```

```python
import functools
import math

import jax
import jax.numpy as jnp
from jax import lax
from jax.experimental import pallas as pl
from jax.experimental.pallas import tpu as pltpu
from jax.sharding import PartitionSpec as P

PANEL = 256
NPANEL = 2
BLOCK = 128
SLAB = 8
EARLY = 0
DEPTH = 256
LANES = 128
NEAR = 3
LARGEST_VECTOR = 6.0
LARGEST_FACTOR = 0.03125
HALF_MAX = 65504.0
NT = (((1,), (1,)), ((), ()))


def dot_once(a, b):
    return lax.dot_general(a, b, NT, preferred_element_type=jnp.float32)


def gram_product(a, b):
    rank = a.shape[1] // 2
    return dot_once(a[:, :rank], b[:, :rank]) * dot_once(a[:, rank:], b[:, rank:])


def unit(size):
    row = lax.broadcasted_iota(jnp.int32, (size, size), 0)
    col = lax.broadcasted_iota(jnp.int32, (size, size), 1)
    return jnp.where(row == col, 1.0, 0.0).astype(jnp.bfloat16)


def split_index(index_row):
    count = index_row.shape[1]
    turned = []
    for part in (index_row % DEPTH, index_row // DEPTH):
        rows = jnp.broadcast_to(part.astype(jnp.float32), (LANES, count)).astype(jnp.bfloat16)
        turned.append(dot_once(unit(count), rows).astype(jnp.int32))
    return turned


def pick_rows(table_ref, index_row, keep):
    width, total = table_ref.shape
    within, run = split_index(index_row)
    place = lax.broadcasted_iota(jnp.int32, within.shape, 1)
    one_hot = jnp.concatenate(
        [jnp.where(within == place + s, 1.0, 0.0) for s in range(0, DEPTH, LANES)], axis=1
    ).astype(jnp.bfloat16)
    each = LANES // width
    runs_at_once = 2 * each
    picked = jnp.zeros(within.shape, jnp.float32)
    for first in range(0, total // DEPTH, runs_at_once):
        if first:
            yield
        runs = jnp.concatenate(
            [table_ref[:, r * DEPTH : (r + 1) * DEPTH] for r in range(first, first + runs_at_once)],
            axis=0,
        )
        found = dot_once(one_hot, runs)
        for half in range(2):
            here = run == first + half * each + place // width
            picked = jnp.where(here, found[:, half * LANES : (half + 1) * LANES], picked)
    out = picked[:, :width]
    for s in range(width, LANES, width):
        out = out + picked[:, s : s + width]
    keep(out.astype(jnp.bfloat16))


def add_unit(block, flag):
    row = lax.broadcasted_iota(jnp.int32, (LANES, LANES), 0)
    col = lax.broadcasted_iota(jnp.int32, (LANES, LANES), 1)
    ones = jnp.where(row == col, flag, 0.0)
    bands = []
    for r in range(0, block.shape[0], LANES):
        parts = []
        for c in range(0, block.shape[1], LANES):
            part = block[r : r + LANES, c : c + LANES]
            parts.append(part + ones if r == c else part)
        bands.append(jnp.concatenate(parts, axis=1))
    return jnp.concatenate(bands, axis=0)


def lanes(x, index):
    return jnp.take_along_axis(x, index, axis=1, mode="promise_in_bounds")


def split_three(x):
    high = x.astype(jnp.bfloat16).astype(jnp.float32)
    rest = x - high
    mid = rest.astype(jnp.bfloat16).astype(jnp.float32)
    return high, mid, rest - mid


def eliminate(block, side):
    size = block.shape[0]
    tiles = size // LANES
    shape = (SLAB, LANES)
    lane = lax.broadcasted_iota(jnp.int32, shape, 1)
    sub = lax.broadcasted_iota(jnp.int32, shape, 0)
    zero = jnp.zeros(shape, jnp.float32)
    identity = unit(size)
    work = [
        [block[s : s + SLAB, i * LANES : (i + 1) * LANES] for i in range(tiles)]
        for s in range(0, size, SLAB)
    ]
    upper, inverse = [], []

    def column(x, at):
        return lanes(x, jnp.full(shape, at, jnp.int32))

    def spread(x, r):
        return jnp.broadcast_to(x[r : r + 1], shape)

    lead = [column(work[0][0], c) for c in range(SLAB)]
    for slab in range(size // SLAB):
        at = SLAB * slab
        here, low = divmod(at, LANES)
        inside = (lane >= low) & (lane < low + SLAB)
        count = min(NEAR, len(work))
        raw = work[0]
        cols = lead
        near = [[column(w[here], low + c) for c in range(SLAB)] for w in work[1:count]]
        if count > 1:
            follow_at, follow_low = divmod(at + SLAB, LANES)
            lead = [column(work[1][follow_at], follow_low + c) for c in range(SLAB)]
            beside = list(near[0])
        rows = list(raw)
        rows[here] = jnp.where(inside, jnp.where(lane - low == sub, 1.0, 0.0), raw[here])
        own = raw[here]
        pivot = spread(cols[0], 0)
        diagonal = pivot
        for j in range(SLAB):
            inv = 1.0 / pivot
            pivots = [spread(cols[c], j) if c > j else None for c in range(SLAB)]
            if j + 1 < SLAB:
                pivot = spread(cols[j + 1], j + 1) - pivots[j + 1] * pivots[j + 1] * inv
                diagonal = jnp.where(sub > j, pivot, diagonal)
            top = [spread(r, j) for r in rows]
            top_own = spread(own, j)
            if j == 0:
                kept, kept_own, inverted = top, top_own, inv
            else:
                kept = [jnp.where(sub >= j, a, b) for a, b in zip(top, kept)]
                kept_own = jnp.where(sub >= j, top_own, kept_own)
                inverted = jnp.where(sub >= j, inv, inverted)
            times = jnp.where(sub == j, 0.0, cols[j] * inv)
            for c in range(j + 1, SLAB):
                cols[c] = cols[c] - times * pivots[c]
            if count > 1:
                times_next = beside[j] * inv
                lead = [a - times_next * spread(beside[j], c) for c, a in enumerate(lead)]
                for c in range(j + 1, SLAB):
                    beside[c] = beside[c] - times_next * pivots[c]
            rows = [r - times * t for r, t in zip(rows, top)]
            own = own - times * top_own
        scale = lax.rsqrt(diagonal)
        factor = [zero] * here + [jnp.where(lane >= low + sub, kept_own * scale, 0.0)]
        factor += [r * scale for r in kept[here + 1 :]]
        back = [r * scale for r in kept[:here]]
        back += [jnp.where(lane < low + SLAB, kept[here] * scale, 0.0)] + [zero] * (tiles - here - 1)
        upper.append(jnp.concatenate(factor, axis=1))
        inverse.append(jnp.concatenate(back, axis=1))
        work = work[1:]
        if work:
            solved = [r * inverted for r in rows]
            work = [
                [jnp.where(inside, 0.0, w) if i == here else w for i, w in enumerate(ws)] for ws in work
            ]
            for t, parts in enumerate(near):
                for i in range(tiles):
                    for c in range(SLAB):
                        work[t][i] = work[t][i] - parts[c] * spread(solved[i], c)
        side()
        if len(work) >= count:
            h, m, l = split_three(jnp.concatenate(raw, axis=1))
            left = jnp.concatenate([h, h, m, m, h, l], axis=0).astype(jnp.bfloat16)
            start = SLAB * (slab + count)
            aligned = start // LANES * LANES
            turned = dot_once(identity[aligned:, :], left).astype(jnp.bfloat16)
            h, m, l = split_three(jnp.concatenate(solved, axis=1))
            right = jnp.concatenate([h, m, h, m, l, h], axis=0).astype(jnp.bfloat16)
            update = lax.dot_general(
                turned, right, (((1,), (0,)), ((), ())), preferred_element_type=jnp.float32
            )
            for t in range(count - 1, len(work)):
                first = SLAB * (slab + 1 + t) - aligned
                for i in range(tiles):
                    work[t][i] = work[t][i] - update[first : first + SLAB, i * LANES : (i + 1) * LANES]
    return jnp.concatenate(upper, axis=0), jnp.concatenate(inverse, axis=0)


def split_pair(x):
    high = x.astype(jnp.bfloat16)
    return high, (x - high.astype(jnp.float32)).astype(jnp.bfloat16)


def as_left(x):
    high, low = split_pair(x)
    return jnp.concatenate([high, high, low], axis=1)


def as_right(x):
    high, low = split_pair(x)
    return jnp.concatenate([high, low, high], axis=1)


def dot_six(a, b):
    h, m, l = [x.astype(jnp.bfloat16) for x in split_three(a)]
    H, M, Lo = [x.astype(jnp.bfloat16) for x in split_three(b)]
    return dot_once(
        jnp.concatenate([h, h, m, m, h, l], axis=1), jnp.concatenate([H, M, H, M, Lo, H], axis=1)
    )


def tile_kernel(
    place_ref, table_ref, first_ref, rows_ref, cols_ref, out_ref,
    lead_ref, vecs_ref, plain_ref, left_ref, right_ref, rest_ref, work_ref, back_ref, lower_ref, found_ref,
):
    height, width = out_ref.shape
    size = work_ref.shape[0]
    steps = size // PANEL
    row_start = place_ref[0]
    col_start = place_ref[1]
    col_chunks = list(range(0, width, PANEL))
    row_chunks = list(range(width, width + height, PANEL))

    def span(panel):
        return slice(panel * PANEL, (panel + 1) * PANEL)

    def wide(panel):
        return slice(panel * 3 * PANEL, (panel + 1) * 3 * PANEL)

    def number(start):
        return row_start + (start - width) if start >= width else col_start + start

    def flag(condition):
        return jnp.where(condition, 1.0, 0.0)

    def gather(start):
        if start < width:
            index = cols_ref[:, start : start + PANEL]
        else:
            index = rows_ref[:, start - width : start - width + PANEL]

        def keep(vecs):
            vecs_ref[start : start + PANEL, :] = vecs

        return pick_rows(table_ref, index, keep)

    def plain(start):
        for p in range(steps):
            if p:
                yield
            block = gram_product(vecs_ref[start : start + PANEL, :], lead_ref[span(p), :])
            plain_ref[start : start + PANEL, span(p)] = add_unit(
                block, flag(number(start) == p * PANEL)
            )

    def schur(start):
        for c in col_chunks:
            if c:
                yield
            block = gram_product(vecs_ref[start : start + PANEL, :], vecs_ref[c : c + PANEL, :])
            out_ref[start - width : start - width + PANEL, c : c + PANEL] = add_unit(
                block, flag(number(start) == number(c))
            )

    def solve(start, panel):
        here = slice(start, start + PANEL)
        source = plain_ref if panel == 0 else rest_ref
        found = dot_once(as_left(source[here, span(panel)]), back_ref[span(panel), :])
        if start < width:
            right_ref[here, wide(panel)] = as_right(found)
        else:
            at = slice(start - width, start - width + PANEL)
            found_ref[at, span(panel)] = found
            left_ref[at, wide(panel)] = as_left(found)
        for later in range(panel + 1, steps):
            yield
            if start < width:
                left = as_left(found)
            else:
                left = left_ref[at, wide(panel)]
            source = plain_ref if panel == 0 else rest_ref
            rest_ref[here, span(later)] = source[here, span(later)] - dot_once(
                left, lower_ref[span(later), wide(panel)]
            )

    def update(start, panel):
        at = slice(start - width, start - width + PANEL)
        below = flag(number(start) >= (panel + 1) * PANEL)
        for c in col_chunks:
            if c:
                yield
            change = dot_once(left_ref[at, wide(panel)], right_ref[c : c + PANEL, wide(panel)])
            out_ref[at, c : c + PANEL] = out_ref[at, c : c + PANEL] - below * change

    def lead_rows(panel):
        def keep(vecs):
            lead_ref[span(panel), :] = vecs

        return pick_rows(table_ref, first_ref[:, span(panel)], keep)

    def lead_block(p, q):
        block = gram_product(lead_ref[span(p), :], lead_ref[span(q), :])
        work_ref[span(p), span(q)] = add_unit(block, 1.0) if p == q else block
        yield

    def finish(pieces):
        for _ in pieces:
            pass

    finish(lead_rows(0))
    finish(lead_block(0, 0))
    for p in range(steps):
        tasks = []
        if p == 0:
            for q in range(1, steps):
                tasks.append(lead_rows(q))
                tasks += [lead_block(q, r) for r in range(q + 1)]
            for start in col_chunks + row_chunks:
                tasks += [gather(start), plain(start)]
            tasks += [schur(start) for start in row_chunks[:EARLY]]
        else:
            tasks += [solve(start, p - 1) for start in col_chunks + row_chunks]
            if p == 1:
                tasks += [schur(start) for start in row_chunks[EARLY:]]
            tasks += [update(start, p - 1) for start in row_chunks]
        counts = len(tasks)
        issued = [0, 0.0]

        def side():
            issued[1] += counts / (PANEL // SLAB)
            while issued[0] < issued[1] - 1e-6 and tasks:
                finish(tasks.pop(0))
                issued[0] += 1

        upper, inverse = eliminate(work_ref[span(p), span(p)], side)
        for rest in tasks:
            finish(rest)
        back_ref[span(p), :] = as_right(inverse)
        below = [dot_six(work_ref[span(q), span(p)], inverse) for q in range(p + 1, steps)]
        for q in range(p + 1, steps):
            lower_ref[span(q), wide(p)] = as_right(below[q - p - 1])
            for r in range(p + 1, q + 1):
                work_ref[span(q), span(r)] = work_ref[span(q), span(r)] - dot_six(
                    below[q - p - 1], below[r - p - 1]
                )
    for start in col_chunks + row_chunks:
        finish(solve(start, steps - 1))
    in_prefix = col_start < size

    @pl.when(in_prefix)
    def _():
        row = lax.broadcasted_iota(jnp.int32, (height, size), 0) + row_start
        col = lax.broadcasted_iota(jnp.int32, (height, size), 1)
        left_alone = row < (col // PANEL) * PANEL
        found_ref[...] = jnp.where(
            left_alone, plain_ref[width:, :], jnp.where(col > row, 0.0, found_ref[...])
        )
        out_ref[...] = found_ref[:, pl.ds(pl.multiple_of(col_start, LANES), width)]

    @pl.when(jnp.logical_not(in_prefix))
    def _():
        for start in row_chunks:
            finish(update(start, steps - 1))


def sum_over(value, axis, depth):
    size = lax.axis_size(axis)
    bound = LARGEST_VECTOR * LARGEST_FACTOR * depth
    scale = 2.0 ** math.floor(math.log2(HALF_MAX / bound))
    value = value * scale
    step = 1
    while step < size:
        sent = lax.reduce_precision(value, 5, 10)
        pairs = [(i, i ^ step) for i in range(size)]
        value = sent + lax.ppermute(sent.astype(jnp.float16), axis, pairs).astype(jnp.float32)
        step *= 2
    return value * (1.0 / scale)


def body(outcome_vectors, u_factor, v_factor, outcome_index):
    cols_n = lax.axis_size("col")
    factors = jnp.concatenate([u_factor, v_factor], axis=0)
    partial_value = lax.dot_general(factors, outcome_vectors, NT, preferred_element_type=jnp.float32)
    width = partial_value.shape[0]
    own_block = sum_over(partial_value, "col", outcome_vectors.shape[1] * cols_n)
    table = lax.all_gather(own_block.astype(jnp.bfloat16), "row", axis=1, tiled=True)
    total = table.shape[1]
    row_height = total // lax.axis_size("row")
    col_width = total // cols_n
    prefix = NPANEL * PANEL
    row_start = lax.axis_index("row") * row_height
    col_start = lax.axis_index("col") * col_width
    index = outcome_index[None, :]
    row_ids = lax.dynamic_slice_in_dim(index, row_start, row_height, 1)
    col_ids = lax.dynamic_slice_in_dim(index, col_start, col_width, 1)
    place = jnp.stack([row_start, col_start]).astype(jnp.int32)
    stack = row_height + col_width
    in_vmem = pl.BlockSpec(memory_space=pltpu.VMEM)
    return pl.pallas_call(
        tile_kernel,
        in_specs=[pl.BlockSpec(memory_space=pltpu.SMEM)] + [in_vmem] * 4,
        out_specs=in_vmem,
        out_shape=jax.ShapeDtypeStruct((row_height, col_width), jnp.float32),
        scratch_shapes=[
            pltpu.VMEM((prefix, width), jnp.bfloat16),
            pltpu.VMEM((stack, width), jnp.bfloat16),
            pltpu.VMEM((stack, prefix), jnp.float32),
            pltpu.VMEM((row_height, 3 * prefix), jnp.bfloat16),
            pltpu.VMEM((col_width, 3 * prefix), jnp.bfloat16),
            pltpu.VMEM((stack, prefix), jnp.float32),
            pltpu.VMEM((prefix, prefix), jnp.float32),
            pltpu.VMEM((prefix, 3 * PANEL), jnp.bfloat16),
            pltpu.VMEM((prefix, 3 * prefix), jnp.bfloat16),
            pltpu.VMEM((row_height, prefix), jnp.float32),
        ],
        compiler_params=pltpu.CompilerParams(vmem_limit_bytes=56 * 2**20),
        name="factor_and_update",
    )(place, table, index[:, :prefix], row_ids, col_ids)


def solution(mesh):
    placed = (P("row", "col"), P(None, "col"), P(None, "col"), P())
    return jax.shard_map(
        body, mesh=mesh, in_specs=placed, out_specs=P("row", "col"), check_vma=False
    )
```

```python
import functools
import math

import jax
import jax.numpy as jnp
from jax import lax
from jax.experimental import pallas as pl
from jax.experimental.pallas import tpu as pltpu
from jax.sharding import PartitionSpec as P

PANEL = 256
NPANEL = 2
BLOCK = 128
SLAB = 8
EARLY = 0
DEPTH = 256
LANES = 128
NEAR = 4
LARGEST_VECTOR = 6.0
LARGEST_FACTOR = 0.03125
HALF_MAX = 65504.0
NT = (((1,), (1,)), ((), ()))


def dot_once(a, b):
    return lax.dot_general(a, b, NT, preferred_element_type=jnp.float32)


def gram_product(a, b):
    rank = a.shape[1] // 2
    return dot_once(a[:, :rank], b[:, :rank]) * dot_once(a[:, rank:], b[:, rank:])


def unit(size):
    row = lax.broadcasted_iota(jnp.int32, (size, size), 0)
    col = lax.broadcasted_iota(jnp.int32, (size, size), 1)
    return jnp.where(row == col, 1.0, 0.0).astype(jnp.bfloat16)


def split_index(index_row):
    count = index_row.shape[1]
    turned = []
    for part in (index_row % DEPTH, index_row // DEPTH):
        rows = jnp.broadcast_to(part.astype(jnp.float32), (LANES, count)).astype(jnp.bfloat16)
        turned.append(dot_once(unit(count), rows).astype(jnp.int32))
    return turned


def pick_rows(table_ref, index_row, keep):
    width, total = table_ref.shape
    within, run = split_index(index_row)
    place = lax.broadcasted_iota(jnp.int32, within.shape, 1)
    one_hot = jnp.concatenate(
        [jnp.where(within == place + s, 1.0, 0.0) for s in range(0, DEPTH, LANES)], axis=1
    ).astype(jnp.bfloat16)
    each = LANES // width
    runs_at_once = 2 * each
    picked = jnp.zeros(within.shape, jnp.float32)
    for first in range(0, total // DEPTH, runs_at_once):
        if first:
            yield
        runs = jnp.concatenate(
            [table_ref[:, r * DEPTH : (r + 1) * DEPTH] for r in range(first, first + runs_at_once)],
            axis=0,
        )
        found = dot_once(one_hot, runs)
        for half in range(2):
            here = run == first + half * each + place // width
            picked = jnp.where(here, found[:, half * LANES : (half + 1) * LANES], picked)
    out = picked[:, :width]
    for s in range(width, LANES, width):
        out = out + picked[:, s : s + width]
    keep(out.astype(jnp.bfloat16))


def add_unit(block, flag):
    row = lax.broadcasted_iota(jnp.int32, (LANES, LANES), 0)
    col = lax.broadcasted_iota(jnp.int32, (LANES, LANES), 1)
    ones = jnp.where(row == col, flag, 0.0)
    bands = []
    for r in range(0, block.shape[0], LANES):
        parts = []
        for c in range(0, block.shape[1], LANES):
            part = block[r : r + LANES, c : c + LANES]
            parts.append(part + ones if r == c else part)
        bands.append(jnp.concatenate(parts, axis=1))
    return jnp.concatenate(bands, axis=0)


def lanes(x, index):
    return jnp.take_along_axis(x, index, axis=1, mode="promise_in_bounds")


def split_three(x):
    high = x.astype(jnp.bfloat16).astype(jnp.float32)
    rest = x - high
    mid = rest.astype(jnp.bfloat16).astype(jnp.float32)
    return high, mid, rest - mid


def eliminate(block, side):
    size = block.shape[0]
    tiles = size // LANES
    shape = (SLAB, LANES)
    lane = lax.broadcasted_iota(jnp.int32, shape, 1)
    sub = lax.broadcasted_iota(jnp.int32, shape, 0)
    zero = jnp.zeros(shape, jnp.float32)
    identity = unit(size)
    work = [
        [block[s : s + SLAB, i * LANES : (i + 1) * LANES] for i in range(tiles)]
        for s in range(0, size, SLAB)
    ]
    upper, inverse = [], []

    def spread(x, r):
        return jnp.broadcast_to(x[r : r + 1], shape)

    def turn(slab_rows, at):
        tile, low = divmod(at, LANES)
        return [lanes(spread(slab_rows[tile], c), low + sub) for c in range(SLAB)]

    for slab in range(size // SLAB):
        at = SLAB * slab
        here, low = divmod(at, LANES)
        inside = (lane >= low) & (lane < low + SLAB)
        count = min(NEAR, len(work))
        raw = work[0]
        cols, *near = [turn(raw, at + SLAB * t) for t in range(count)]
        rows = list(raw)
        rows[here] = jnp.where(inside, jnp.where(lane - low == sub, 1.0, 0.0), raw[here])
        own = raw[here]
        pivot = spread(cols[0], 0)
        diagonal = pivot
        for j in range(SLAB):
            inv = 1.0 / pivot
            pivots = [spread(cols[c], j) if c > j else None for c in range(SLAB)]
            if j + 1 < SLAB:
                pivot = spread(cols[j + 1], j + 1) - pivots[j + 1] * pivots[j + 1] * inv
                diagonal = jnp.where(sub > j, pivot, diagonal)
            top = [spread(r, j) for r in rows]
            top_own = spread(own, j)
            if j == 0:
                kept, kept_own, inverted = top, top_own, inv
            else:
                kept = [jnp.where(sub >= j, a, b) for a, b in zip(top, kept)]
                kept_own = jnp.where(sub >= j, top_own, kept_own)
                inverted = jnp.where(sub >= j, inv, inverted)
            times = jnp.where(sub == j, 0.0, cols[j] * inv)
            for c in range(j + 1, SLAB):
                cols[c] = cols[c] - times * pivots[c]
            rows = [r - times * t for r, t in zip(rows, top)]
            own = own - times * top_own
        scale = lax.rsqrt(diagonal)
        factor = [zero] * here + [jnp.where(lane >= low + sub, kept_own * scale, 0.0)]
        factor += [r * scale for r in kept[here + 1 :]]
        back = [r * scale for r in kept[:here]]
        back += [jnp.where(lane < low + SLAB, kept[here] * scale, 0.0)] + [zero] * (tiles - here - 1)
        upper.append(jnp.concatenate(factor, axis=1))
        inverse.append(jnp.concatenate(back, axis=1))
        work = work[1:]
        if work:
            solved = [r * inverted for r in rows]
            work = [
                [jnp.where(inside, 0.0, w) if i == here else w for i, w in enumerate(ws)] for ws in work
            ]
            for t, parts in enumerate(near):
                for i in range(tiles):
                    for c in range(SLAB):
                        work[t][i] = work[t][i] - parts[c] * spread(solved[i], c)
        side()
        if len(work) >= count:
            h, m, l = split_three(jnp.concatenate(raw, axis=1))
            left = jnp.concatenate([h, h, m, m, h, l], axis=0).astype(jnp.bfloat16)
            start = SLAB * (slab + count)
            aligned = start // LANES * LANES
            turned = dot_once(identity[aligned:, :], left).astype(jnp.bfloat16)
            h, m, l = split_three(jnp.concatenate(solved, axis=1))
            right = jnp.concatenate([h, m, h, m, l, h], axis=0).astype(jnp.bfloat16)
            update = lax.dot_general(
                turned, right, (((1,), (0,)), ((), ())), preferred_element_type=jnp.float32
            )
            for t in range(count - 1, len(work)):
                first = SLAB * (slab + 1 + t) - aligned
                for i in range(tiles):
                    work[t][i] = work[t][i] - update[first : first + SLAB, i * LANES : (i + 1) * LANES]
    return jnp.concatenate(upper, axis=0), jnp.concatenate(inverse, axis=0)


def split_pair(x):
    high = x.astype(jnp.bfloat16)
    return high, (x - high.astype(jnp.float32)).astype(jnp.bfloat16)


def as_left(x):
    high, low = split_pair(x)
    return jnp.concatenate([high, high, low], axis=1)


def as_right(x):
    high, low = split_pair(x)
    return jnp.concatenate([high, low, high], axis=1)


def dot_six(a, b):
    h, m, l = [x.astype(jnp.bfloat16) for x in split_three(a)]
    H, M, Lo = [x.astype(jnp.bfloat16) for x in split_three(b)]
    return dot_once(
        jnp.concatenate([h, h, m, m, h, l], axis=1), jnp.concatenate([H, M, H, M, Lo, H], axis=1)
    )


def tile_kernel(
    place_ref, table_ref, first_ref, rows_ref, cols_ref, out_ref,
    lead_ref, vecs_ref, plain_ref, left_ref, right_ref, rest_ref, work_ref, back_ref, lower_ref, found_ref,
):
    height, width = out_ref.shape
    size = work_ref.shape[0]
    steps = size // PANEL
    row_start = place_ref[0]
    col_start = place_ref[1]
    col_chunks = list(range(0, width, PANEL))
    row_chunks = list(range(width, width + height, PANEL))

    def span(panel):
        return slice(panel * PANEL, (panel + 1) * PANEL)

    def wide(panel):
        return slice(panel * 3 * PANEL, (panel + 1) * 3 * PANEL)

    def number(start):
        return row_start + (start - width) if start >= width else col_start + start

    def flag(condition):
        return jnp.where(condition, 1.0, 0.0)

    def gather(start):
        if start < width:
            index = cols_ref[:, start : start + PANEL]
        else:
            index = rows_ref[:, start - width : start - width + PANEL]

        def keep(vecs):
            vecs_ref[start : start + PANEL, :] = vecs

        return pick_rows(table_ref, index, keep)

    def plain(start):
        for p in range(steps):
            if p:
                yield
            block = gram_product(vecs_ref[start : start + PANEL, :], lead_ref[span(p), :])
            plain_ref[start : start + PANEL, span(p)] = add_unit(
                block, flag(number(start) == p * PANEL)
            )

    def schur(start):
        for c in col_chunks:
            if c:
                yield
            block = gram_product(vecs_ref[start : start + PANEL, :], vecs_ref[c : c + PANEL, :])
            out_ref[start - width : start - width + PANEL, c : c + PANEL] = add_unit(
                block, flag(number(start) == number(c))
            )

    def solve(start, panel):
        here = slice(start, start + PANEL)
        source = plain_ref if panel == 0 else rest_ref
        found = dot_once(as_left(source[here, span(panel)]), back_ref[span(panel), :])
        if start < width:
            right_ref[here, wide(panel)] = as_right(found)
        else:
            at = slice(start - width, start - width + PANEL)
            found_ref[at, span(panel)] = found
            left_ref[at, wide(panel)] = as_left(found)
        for later in range(panel + 1, steps):
            yield
            if start < width:
                left = as_left(found)
            else:
                left = left_ref[at, wide(panel)]
            source = plain_ref if panel == 0 else rest_ref
            rest_ref[here, span(later)] = source[here, span(later)] - dot_once(
                left, lower_ref[span(later), wide(panel)]
            )

    def update(start, panel):
        at = slice(start - width, start - width + PANEL)
        below = flag(number(start) >= (panel + 1) * PANEL)
        for c in col_chunks:
            if c:
                yield
            change = dot_once(left_ref[at, wide(panel)], right_ref[c : c + PANEL, wide(panel)])
            out_ref[at, c : c + PANEL] = out_ref[at, c : c + PANEL] - below * change

    def lead_rows(panel):
        def keep(vecs):
            lead_ref[span(panel), :] = vecs

        return pick_rows(table_ref, first_ref[:, span(panel)], keep)

    def lead_block(p, q):
        block = gram_product(lead_ref[span(p), :], lead_ref[span(q), :])
        work_ref[span(p), span(q)] = add_unit(block, 1.0) if p == q else block
        yield

    def finish(pieces):
        for _ in pieces:
            pass

    finish(lead_rows(0))
    finish(lead_block(0, 0))
    for p in range(steps):
        tasks = []
        if p == 0:
            for q in range(1, steps):
                tasks.append(lead_rows(q))
                tasks += [lead_block(q, r) for r in range(q + 1)]
            for start in col_chunks + row_chunks:
                tasks += [gather(start), plain(start)]
            tasks += [schur(start) for start in row_chunks[:EARLY]]
        else:
            tasks += [solve(start, p - 1) for start in col_chunks + row_chunks]
            if p == 1:
                tasks += [schur(start) for start in row_chunks[EARLY:]]
            tasks += [update(start, p - 1) for start in row_chunks]
        counts = len(tasks)
        issued = [0, 0.0]

        def side():
            issued[1] += counts / (PANEL // SLAB)
            while issued[0] < issued[1] - 1e-6 and tasks:
                finish(tasks.pop(0))
                issued[0] += 1

        upper, inverse = eliminate(work_ref[span(p), span(p)], side)
        for rest in tasks:
            finish(rest)
        back_ref[span(p), :] = as_right(inverse)
        below = [dot_six(work_ref[span(q), span(p)], inverse) for q in range(p + 1, steps)]
        for q in range(p + 1, steps):
            lower_ref[span(q), wide(p)] = as_right(below[q - p - 1])
            for r in range(p + 1, q + 1):
                work_ref[span(q), span(r)] = work_ref[span(q), span(r)] - dot_six(
                    below[q - p - 1], below[r - p - 1]
                )
    for start in col_chunks + row_chunks:
        finish(solve(start, steps - 1))
    in_prefix = col_start < size

    @pl.when(in_prefix)
    def _():
        row = lax.broadcasted_iota(jnp.int32, (height, size), 0) + row_start
        col = lax.broadcasted_iota(jnp.int32, (height, size), 1)
        left_alone = row < (col // PANEL) * PANEL
        found_ref[...] = jnp.where(
            left_alone, plain_ref[width:, :], jnp.where(col > row, 0.0, found_ref[...])
        )
        out_ref[...] = found_ref[:, pl.ds(pl.multiple_of(col_start, LANES), width)]

    @pl.when(jnp.logical_not(in_prefix))
    def _():
        for start in row_chunks:
            finish(update(start, steps - 1))


def sum_over(value, axis, depth):
    size = lax.axis_size(axis)
    bound = LARGEST_VECTOR * LARGEST_FACTOR * depth
    scale = 2.0 ** math.floor(math.log2(HALF_MAX / bound))
    value = value * scale
    step = 1
    while step < size:
        sent = lax.reduce_precision(value, 5, 10)
        pairs = [(i, i ^ step) for i in range(size)]
        value = sent + lax.ppermute(sent.astype(jnp.float16), axis, pairs).astype(jnp.float32)
        step *= 2
    return value * (1.0 / scale)


def body(outcome_vectors, u_factor, v_factor, outcome_index):
    cols_n = lax.axis_size("col")
    factors = jnp.concatenate([u_factor, v_factor], axis=0)
    partial_value = lax.dot_general(factors, outcome_vectors, NT, preferred_element_type=jnp.float32)
    width = partial_value.shape[0]
    own_block = sum_over(partial_value, "col", outcome_vectors.shape[1] * cols_n)
    table = lax.all_gather(own_block.astype(jnp.bfloat16), "row", axis=1, tiled=True)
    total = table.shape[1]
    row_height = total // lax.axis_size("row")
    col_width = total // cols_n
    prefix = NPANEL * PANEL
    row_start = lax.axis_index("row") * row_height
    col_start = lax.axis_index("col") * col_width
    index = outcome_index[None, :]
    row_ids = lax.dynamic_slice_in_dim(index, row_start, row_height, 1)
    col_ids = lax.dynamic_slice_in_dim(index, col_start, col_width, 1)
    place = jnp.stack([row_start, col_start]).astype(jnp.int32)
    stack = row_height + col_width
    in_vmem = pl.BlockSpec(memory_space=pltpu.VMEM)
    return pl.pallas_call(
        tile_kernel,
        in_specs=[pl.BlockSpec(memory_space=pltpu.SMEM)] + [in_vmem] * 4,
        out_specs=in_vmem,
        out_shape=jax.ShapeDtypeStruct((row_height, col_width), jnp.float32),
        scratch_shapes=[
            pltpu.VMEM((prefix, width), jnp.bfloat16),
            pltpu.VMEM((stack, width), jnp.bfloat16),
            pltpu.VMEM((stack, prefix), jnp.float32),
            pltpu.VMEM((row_height, 3 * prefix), jnp.bfloat16),
            pltpu.VMEM((col_width, 3 * prefix), jnp.bfloat16),
            pltpu.VMEM((stack, prefix), jnp.float32),
            pltpu.VMEM((prefix, prefix), jnp.float32),
            pltpu.VMEM((prefix, 3 * PANEL), jnp.bfloat16),
            pltpu.VMEM((prefix, 3 * prefix), jnp.bfloat16),
            pltpu.VMEM((row_height, prefix), jnp.float32),
        ],
        compiler_params=pltpu.CompilerParams(vmem_limit_bytes=56 * 2**20),
        name="factor_and_update",
    )(place, table, index[:, :prefix], row_ids, col_ids)


def solution(mesh):
    placed = (P("row", "col"), P(None, "col"), P(None, "col"), P())
    return jax.shard_map(
        body, mesh=mesh, in_specs=placed, out_specs=P("row", "col"), check_vma=False
    )
```

```python
import functools
import math

import jax
import jax.numpy as jnp
from jax import lax
from jax.experimental import pallas as pl
from jax.experimental.pallas import tpu as pltpu
from jax.sharding import PartitionSpec as P

PANEL = 256
NPANEL = 2
BLOCK = 128
SLAB = 8
EARLY = 0
DEPTH = 256
LANES = 128
NEAR = 4
LARGEST_VECTOR = 6.0
LARGEST_FACTOR = 0.03125
HALF_MAX = 65504.0
NT = (((1,), (1,)), ((), ()))


def dot_once(a, b):
    return lax.dot_general(a, b, NT, preferred_element_type=jnp.float32)


def gram_product(a, b):
    rank = a.shape[1] // 2
    return dot_once(a[:, :rank], b[:, :rank]) * dot_once(a[:, rank:], b[:, rank:])


def unit(size):
    row = lax.broadcasted_iota(jnp.int32, (size, size), 0)
    col = lax.broadcasted_iota(jnp.int32, (size, size), 1)
    return jnp.where(row == col, 1.0, 0.0).astype(jnp.bfloat16)


def split_index(index_row):
    count = index_row.shape[1]
    turned = []
    for part in (index_row % DEPTH, index_row // DEPTH):
        rows = jnp.broadcast_to(part.astype(jnp.float32), (LANES, count)).astype(jnp.bfloat16)
        turned.append(dot_once(unit(count), rows).astype(jnp.int32))
    return turned


def pick_rows(table_ref, index_row, keep):
    width, total = table_ref.shape
    within, run = split_index(index_row)
    place = lax.broadcasted_iota(jnp.int32, within.shape, 1)
    one_hot = jnp.concatenate(
        [jnp.where(within == place + s, 1.0, 0.0) for s in range(0, DEPTH, LANES)], axis=1
    ).astype(jnp.bfloat16)
    each = LANES // width
    runs_at_once = 2 * each
    picked = jnp.zeros(within.shape, jnp.float32)
    for first in range(0, total // DEPTH, runs_at_once):
        if first:
            yield
        runs = jnp.concatenate(
            [table_ref[:, r * DEPTH : (r + 1) * DEPTH] for r in range(first, first + runs_at_once)],
            axis=0,
        )
        found = dot_once(one_hot, runs)
        for half in range(2):
            here = run == first + half * each + place // width
            picked = jnp.where(here, found[:, half * LANES : (half + 1) * LANES], picked)
    out = picked[:, :width]
    for s in range(width, LANES, width):
        out = out + picked[:, s : s + width]
    keep(out.astype(jnp.bfloat16))


def add_unit(block, flag):
    row = lax.broadcasted_iota(jnp.int32, (LANES, LANES), 0)
    col = lax.broadcasted_iota(jnp.int32, (LANES, LANES), 1)
    ones = jnp.where(row == col, flag, 0.0)
    bands = []
    for r in range(0, block.shape[0], LANES):
        parts = []
        for c in range(0, block.shape[1], LANES):
            part = block[r : r + LANES, c : c + LANES]
            parts.append(part + ones if r == c else part)
        bands.append(jnp.concatenate(parts, axis=1))
    return jnp.concatenate(bands, axis=0)


def lanes(x, index):
    return jnp.take_along_axis(x, index, axis=1, mode="promise_in_bounds")


def split_three(x):
    high = x.astype(jnp.bfloat16).astype(jnp.float32)
    rest = x - high
    mid = rest.astype(jnp.bfloat16).astype(jnp.float32)
    return high, mid, rest - mid


def eliminate(block, side):
    size = block.shape[0]
    tiles = size // LANES
    shape = (SLAB, LANES)
    lane = lax.broadcasted_iota(jnp.int32, shape, 1)
    sub = lax.broadcasted_iota(jnp.int32, shape, 0)
    zero = jnp.zeros(shape, jnp.float32)
    identity = unit(size)
    work = [
        [block[s : s + SLAB, i * LANES : (i + 1) * LANES] for i in range(tiles)]
        for s in range(0, size, SLAB)
    ]
    upper, inverse = [], []

    def spread(x, r):
        return jnp.broadcast_to(x[r : r + 1], shape)

    def turn(slab_rows, at):
        tile, low = divmod(at, LANES)
        return [lanes(spread(slab_rows[tile], c), low + sub) for c in range(SLAB)]

    for slab in range(size // SLAB):
        at = SLAB * slab
        here, low = divmod(at, LANES)
        inside = (lane >= low) & (lane < low + SLAB)
        count = min(NEAR, len(work))
        raw = work[0]
        cols, *near = [turn(raw, at + SLAB * t) for t in range(count)]
        rows = list(raw)
        rows[here] = jnp.where(inside, jnp.where(lane - low == sub, 1.0, 0.0), raw[here])
        own = raw[here]
        pivot = spread(cols[0], 0)
        diagonal = pivot
        for j in range(SLAB):
            inv = 1.0 / pivot
            pivots = [spread(cols[c], j) if c > j else None for c in range(SLAB)]
            if j + 1 < SLAB:
                pivot = spread(cols[j + 1], j + 1) - pivots[j + 1] * pivots[j + 1] * inv
                diagonal = jnp.where(sub > j, pivot, diagonal)
            top = [spread(r, j) for r in rows]
            top_own = spread(own, j)
            if j == 0:
                kept, kept_own, inverted = top, top_own, inv
            else:
                kept = [jnp.where(sub >= j, a, b) for a, b in zip(top, kept)]
                kept_own = jnp.where(sub >= j, top_own, kept_own)
                inverted = jnp.where(sub >= j, inv, inverted)
            times = jnp.where(sub == j, 0.0, cols[j] * inv)
            for c in range(j + 1, SLAB):
                cols[c] = cols[c] - times * pivots[c]
            rows = [r - times * t for r, t in zip(rows, top)]
            own = own - times * top_own
        scale = lax.rsqrt(diagonal)
        factor = [zero] * here + [jnp.where(lane >= low + sub, kept_own * scale, 0.0)]
        factor += [r * scale for r in kept[here + 1 :]]
        back = [r * scale for r in kept[:here]]
        back += [jnp.where(lane < low + SLAB, kept[here] * scale, 0.0)] + [zero] * (tiles - here - 1)
        upper.append(jnp.concatenate(factor, axis=1))
        inverse.append(jnp.concatenate(back, axis=1))
        work = work[1:]
        if work:
            solved = [r * inverted for r in rows]
            work = [
                [jnp.where(inside, 0.0, w) if i == here else w for i, w in enumerate(ws)] for ws in work
            ]
            for t, parts in enumerate(near):
                for i in range(tiles):
                    terms = [parts[c] * spread(solved[i], c) for c in range(SLAB)]
                    while len(terms) > 1:
                        terms = [a + b for a, b in zip(terms[::2], terms[1::2])]
                    work[t][i] = work[t][i] - terms[0]
        side()
        if len(work) >= count:
            h, m, l = split_three(jnp.concatenate(raw, axis=1))
            left = jnp.concatenate([h, h, m, m, h, l], axis=0).astype(jnp.bfloat16)
            start = SLAB * (slab + count)
            aligned = start // LANES * LANES
            turned = dot_once(identity[aligned:, :], left).astype(jnp.bfloat16)
            h, m, l = split_three(jnp.concatenate(solved, axis=1))
            right = jnp.concatenate([h, m, h, m, l, h], axis=0).astype(jnp.bfloat16)
            update = lax.dot_general(
                turned, right, (((1,), (0,)), ((), ())), preferred_element_type=jnp.float32
            )
            for t in range(count - 1, len(work)):
                first = SLAB * (slab + 1 + t) - aligned
                for i in range(tiles):
                    work[t][i] = work[t][i] - update[first : first + SLAB, i * LANES : (i + 1) * LANES]
    return jnp.concatenate(upper, axis=0), jnp.concatenate(inverse, axis=0)


def split_pair(x):
    high = x.astype(jnp.bfloat16)
    return high, (x - high.astype(jnp.float32)).astype(jnp.bfloat16)


def as_left(x):
    high, low = split_pair(x)
    return jnp.concatenate([high, high, low], axis=1)


def as_right(x):
    high, low = split_pair(x)
    return jnp.concatenate([high, low, high], axis=1)


def dot_six(a, b):
    h, m, l = [x.astype(jnp.bfloat16) for x in split_three(a)]
    H, M, Lo = [x.astype(jnp.bfloat16) for x in split_three(b)]
    return dot_once(
        jnp.concatenate([h, h, m, m, h, l], axis=1), jnp.concatenate([H, M, H, M, Lo, H], axis=1)
    )


def tile_kernel(
    place_ref, table_ref, first_ref, rows_ref, cols_ref, out_ref,
    lead_ref, vecs_ref, plain_ref, left_ref, right_ref, rest_ref, work_ref, back_ref, lower_ref, found_ref,
):
    height, width = out_ref.shape
    size = work_ref.shape[0]
    steps = size // PANEL
    row_start = place_ref[0]
    col_start = place_ref[1]
    col_chunks = list(range(0, width, PANEL))
    row_chunks = list(range(width, width + height, PANEL))

    def span(panel):
        return slice(panel * PANEL, (panel + 1) * PANEL)

    def wide(panel):
        return slice(panel * 3 * PANEL, (panel + 1) * 3 * PANEL)

    def number(start):
        return row_start + (start - width) if start >= width else col_start + start

    def flag(condition):
        return jnp.where(condition, 1.0, 0.0)

    def gather(start):
        if start < width:
            index = cols_ref[:, start : start + PANEL]
        else:
            index = rows_ref[:, start - width : start - width + PANEL]

        def keep(vecs):
            vecs_ref[start : start + PANEL, :] = vecs

        return pick_rows(table_ref, index, keep)

    def plain(start):
        for p in range(steps):
            if p:
                yield
            block = gram_product(vecs_ref[start : start + PANEL, :], lead_ref[span(p), :])
            plain_ref[start : start + PANEL, span(p)] = add_unit(
                block, flag(number(start) == p * PANEL)
            )

    def schur(start):
        for c in col_chunks:
            if c:
                yield
            block = gram_product(vecs_ref[start : start + PANEL, :], vecs_ref[c : c + PANEL, :])
            out_ref[start - width : start - width + PANEL, c : c + PANEL] = add_unit(
                block, flag(number(start) == number(c))
            )

    def solve(start, panel):
        here = slice(start, start + PANEL)
        source = plain_ref if panel == 0 else rest_ref
        found = dot_once(as_left(source[here, span(panel)]), back_ref[span(panel), :])
        if start < width:
            right_ref[here, wide(panel)] = as_right(found)
        else:
            at = slice(start - width, start - width + PANEL)
            found_ref[at, span(panel)] = found
            left_ref[at, wide(panel)] = as_left(found)
        for later in range(panel + 1, steps):
            yield
            if start < width:
                left = as_left(found)
            else:
                left = left_ref[at, wide(panel)]
            source = plain_ref if panel == 0 else rest_ref
            rest_ref[here, span(later)] = source[here, span(later)] - dot_once(
                left, lower_ref[span(later), wide(panel)]
            )

    def update(start, panel):
        at = slice(start - width, start - width + PANEL)
        below = flag(number(start) >= (panel + 1) * PANEL)
        for c in col_chunks:
            if c:
                yield
            change = dot_once(left_ref[at, wide(panel)], right_ref[c : c + PANEL, wide(panel)])
            out_ref[at, c : c + PANEL] = out_ref[at, c : c + PANEL] - below * change

    def lead_rows(panel):
        def keep(vecs):
            lead_ref[span(panel), :] = vecs

        return pick_rows(table_ref, first_ref[:, span(panel)], keep)

    def lead_block(p, q):
        block = gram_product(lead_ref[span(p), :], lead_ref[span(q), :])
        work_ref[span(p), span(q)] = add_unit(block, 1.0) if p == q else block
        yield

    def finish(pieces):
        for _ in pieces:
            pass

    finish(lead_rows(0))
    finish(lead_block(0, 0))
    for p in range(steps):
        tasks = []
        if p == 0:
            for q in range(1, steps):
                tasks.append(lead_rows(q))
                tasks += [lead_block(q, r) for r in range(q + 1)]
            for start in col_chunks + row_chunks:
                tasks += [gather(start), plain(start)]
            tasks += [schur(start) for start in row_chunks[:EARLY]]
        else:
            tasks += [solve(start, p - 1) for start in col_chunks + row_chunks]
            if p == 1:
                tasks += [schur(start) for start in row_chunks[EARLY:]]
            tasks += [update(start, p - 1) for start in row_chunks]
        counts = len(tasks)
        issued = [0, 0.0]

        def side():
            issued[1] += counts / (PANEL // SLAB)
            while issued[0] < issued[1] - 1e-6 and tasks:
                finish(tasks.pop(0))
                issued[0] += 1

        upper, inverse = eliminate(work_ref[span(p), span(p)], side)
        for rest in tasks:
            finish(rest)
        back_ref[span(p), :] = as_right(inverse)
        below = [dot_six(work_ref[span(q), span(p)], inverse) for q in range(p + 1, steps)]
        for q in range(p + 1, steps):
            lower_ref[span(q), wide(p)] = as_right(below[q - p - 1])
            for r in range(p + 1, q + 1):
                work_ref[span(q), span(r)] = work_ref[span(q), span(r)] - dot_six(
                    below[q - p - 1], below[r - p - 1]
                )
    for start in col_chunks + row_chunks:
        finish(solve(start, steps - 1))
    in_prefix = col_start < size

    @pl.when(in_prefix)
    def _():
        row = lax.broadcasted_iota(jnp.int32, (height, size), 0) + row_start
        col = lax.broadcasted_iota(jnp.int32, (height, size), 1)
        left_alone = row < (col // PANEL) * PANEL
        found_ref[...] = jnp.where(
            left_alone, plain_ref[width:, :], jnp.where(col > row, 0.0, found_ref[...])
        )
        out_ref[...] = found_ref[:, pl.ds(pl.multiple_of(col_start, LANES), width)]

    @pl.when(jnp.logical_not(in_prefix))
    def _():
        for start in row_chunks:
            finish(update(start, steps - 1))


def sum_over(value, axis, depth):
    size = lax.axis_size(axis)
    bound = LARGEST_VECTOR * LARGEST_FACTOR * depth
    scale = 2.0 ** math.floor(math.log2(HALF_MAX / bound))
    value = value * scale
    step = 1
    while step < size:
        sent = lax.reduce_precision(value, 5, 10)
        pairs = [(i, i ^ step) for i in range(size)]
        value = sent + lax.ppermute(sent.astype(jnp.float16), axis, pairs).astype(jnp.float32)
        step *= 2
    return value * (1.0 / scale)


def body(outcome_vectors, u_factor, v_factor, outcome_index):
    cols_n = lax.axis_size("col")
    factors = jnp.concatenate([u_factor, v_factor], axis=0)
    partial_value = lax.dot_general(factors, outcome_vectors, NT, preferred_element_type=jnp.float32)
    width = partial_value.shape[0]
    own_block = sum_over(partial_value, "col", outcome_vectors.shape[1] * cols_n)
    table = lax.all_gather(own_block.astype(jnp.bfloat16), "row", axis=1, tiled=True)
    total = table.shape[1]
    row_height = total // lax.axis_size("row")
    col_width = total // cols_n
    prefix = NPANEL * PANEL
    row_start = lax.axis_index("row") * row_height
    col_start = lax.axis_index("col") * col_width
    index = outcome_index[None, :]
    row_ids = lax.dynamic_slice_in_dim(index, row_start, row_height, 1)
    col_ids = lax.dynamic_slice_in_dim(index, col_start, col_width, 1)
    place = jnp.stack([row_start, col_start]).astype(jnp.int32)
    stack = row_height + col_width
    in_vmem = pl.BlockSpec(memory_space=pltpu.VMEM)
    return pl.pallas_call(
        tile_kernel,
        in_specs=[pl.BlockSpec(memory_space=pltpu.SMEM)] + [in_vmem] * 4,
        out_specs=in_vmem,
        out_shape=jax.ShapeDtypeStruct((row_height, col_width), jnp.float32),
        scratch_shapes=[
            pltpu.VMEM((prefix, width), jnp.bfloat16),
            pltpu.VMEM((stack, width), jnp.bfloat16),
            pltpu.VMEM((stack, prefix), jnp.float32),
            pltpu.VMEM((row_height, 3 * prefix), jnp.bfloat16),
            pltpu.VMEM((col_width, 3 * prefix), jnp.bfloat16),
            pltpu.VMEM((stack, prefix), jnp.float32),
            pltpu.VMEM((prefix, prefix), jnp.float32),
            pltpu.VMEM((prefix, 3 * PANEL), jnp.bfloat16),
            pltpu.VMEM((prefix, 3 * prefix), jnp.bfloat16),
            pltpu.VMEM((row_height, prefix), jnp.float32),
        ],
        compiler_params=pltpu.CompilerParams(vmem_limit_bytes=56 * 2**20),
        name="factor_and_update",
    )(place, table, index[:, :prefix], row_ids, col_ids)


def solution(mesh):
    placed = (P("row", "col"), P(None, "col"), P(None, "col"), P())
    return jax.shard_map(
        body, mesh=mesh, in_specs=placed, out_specs=P("row", "col"), check_vma=False
    )
```
